512 devices in a mesh: ctx: 64 (over y, z_hi, x), tp: 8 (over z_lo, core).
Axes of the slice: x: 4, y: 8, z: 8 (z_hi: 2, z_lo: 4; z = z_hi * 4 + z_lo), core: 2. Of those that a mesh axis runs over, the one named last changes fastest.
Arguments:
- queries: bfloat16 [8192, 4096], P('ctx', 'tp'), may hold values from -5 to 5
- keys: bfloat16 [8192, 1024], P('ctx', 'tp'), may hold values from -5 to 5
- values: bfloat16 [8192, 1024], P('ctx', 'tp'), may hold values from -6 to 6
- out_grad: bfloat16 [8192, 4096], P('ctx', 'tp'), may hold values from -6 to 6
- features: bfloat16 [8192, 4096], P('ctx'), may hold values from -6 to 6
- segment_ids: int32 [8192], replicated, may hold values from 0 to 15, never falling along the last dimension, each value on 1 to 6144 neighbouring positions
Outputs:
- query_grads: bfloat16 [8192, 4096], P('ctx', 'tp')
- weight_grad: float32 [4096, 1024], P('tp')
The draws below stay inside these ranges and needn't reach their ends.
Inputs may be any that keep to these rules, and one draw needn't show every extreme that they name: `segment_ids`: never falling along the sequence; each document has 1 to 6144 tokens and one has exactly 6144.
All inputs are finite; a program needn't handle non-finite values.
Results may differ from the reference program's by a relative error of at most 0.024.
Values may be sent and summed in bfloat16 or wider, within the bound.
No kernel may reach another device: no remote copies, remote signals or barrier semaphores. Data moves between devices by JAX's collectives and lax.ppermute only.
A program may use at most 64 MiB of HBM per device.

```python
import math
import jax
import jax.numpy as jnp
import numpy as np
from jax import lax

QH = 32
KVH = 8
HD = 128
DX = 4096
SEGS = 16
TOKENS = 8192
MOST = 6144


def draw_queries(key, part):
    key = jax.random.fold_in(key, 3)
    return jnp.clip(1.6 * jax.random.normal(key, (TOKENS, QH * HD), jnp.float32), -5.0, 5.0).astype(jnp.bfloat16)


def draw_keys(key, part):
    key = jax.random.fold_in(key, 4)
    return jnp.clip(1.6 * jax.random.normal(key, (TOKENS, KVH * HD), jnp.float32), -5.0, 5.0).astype(jnp.bfloat16)


def level_of(rng, extent, cuts, least, top_value):
    loudness, own = 1.0, jax.random.fold_in(rng, 6)
    for axis_at, parts in cuts:
        draws = jnp.exp(jax.random.uniform(jax.random.fold_in(own, axis_at), (parts,), jnp.float32, least / len(cuts), top_value / len(cuts)))
        loudness = loudness * jnp.repeat(draws, extent[axis_at] // parts).reshape([-1 if axis == axis_at else 1 for axis in range(len(extent))])
    return loudness


def length_profile(number_of, total, bound, lean):
    weights = [(1 << 20) // math.isqrt(rank ** lean) + 1 for rank in range(2, number_of + 1)]
    spare, counts = total - bound - (number_of - 1), [1] * (number_of - 1)
    while spare > 0:
        candidates = [i for i in range(number_of - 1) if counts[i] < bound]
        mass, budget = sum([weights[i] for i in candidates]), spare
        for i in candidates:
            addition = min(bound - counts[i], max(1, budget * weights[i] // mass), spare)
            counts[i] = counts[i] + addition
            spare = spare - addition
    return np.array([bound] + counts)


def ragged_sizes(rng, number_of, total, limit, lean):
    if number_of == 2:
        one = jax.random.randint(rng, (), max(1, total - limit), min(limit, total - 1) + 1)
        return jnp.stack([one, total - one])
    sizes = jnp.asarray(length_profile(number_of, total, limit, lean), jnp.int32)
    twos = (number_of - 1) // 2
    donor, receiver = sizes[1:1 + 2 * twos:2], sizes[2:2 + 2 * twos:2]
    slack = jnp.minimum(donor - 1, limit - receiver)
    moved = jax.random.randint(jax.random.fold_in(rng, 1), (twos,), 0, 1 << 20) % (slack + 1)
    sizes = sizes.at[1:1 + 2 * twos:2].set(donor - moved).at[2:2 + 2 * twos:2].set(receiver + moved)
    return sizes[jax.random.permutation(jax.random.fold_in(rng, 2), number_of)]


def scatter_about(stream_key, shape, scale, limit, cuts=(), held_as=jnp.bfloat16):
    result = jax.random.normal(stream_key, shape, jnp.float32) * scale
    if len(cuts) > 0:
        result = level_of(stream_key, shape, cuts, -0.22, 0.18) * result
    return jnp.clip(result, min=-limit, max=limit).astype(held_as)


def setup_inputs(seed: int = 0) -> dict:
    key_list = jax.random.split(jax.random.key(seed), 7)
    queries = draw_queries(jax.random.fold_in(key_list[6], 71), 0)
    keys = draw_keys(jax.random.fold_in(key_list[6], 71), 0)
    values = scatter_about(key_list[2], (TOKENS, KVH * HD), 1.0, 6.0, ((0, 64), (1, 8)))
    out_grad = scatter_about(key_list[3], (TOKENS, QH * HD), 1.0, 6.0, ((0, 64), (1, 8)))
    features = scatter_about(key_list[4], (TOKENS, DX), 1.0, 6.0, ((0, 64),))
    segment_ids = jnp.searchsorted(jnp.cumsum(ragged_sizes(key_list[5], SEGS, TOKENS, MOST, 2)), jnp.arange(TOKENS), side="right").astype(jnp.int32)
    return {"queries": queries, "keys": keys, "values": values, "out_grad": out_grad, "features": features, "segment_ids": segment_ids}


def reference(queries, keys, values, out_grad, features, segment_ids):
    group = QH // KVH
    scale = HD ** (-0.5)
    block = math.gcd(TOKENS, 256)
    query_heads = queries.astype(jnp.float32).reshape(TOKENS, KVH, group, HD)
    grad_heads = out_grad.astype(jnp.float32).reshape(TOKENS, KVH, group, HD)
    key_heads = keys.astype(jnp.float32).reshape(TOKENS, KVH, HD)
    value_heads = values.astype(jnp.float32).reshape(TOKENS, KVH, HD)
    positions = jnp.arange(TOKENS, dtype=jnp.int32)

    def step(value_sum, start):
        query_block = lax.dynamic_slice_in_dim(query_heads, start, block, 0)
        grad_block = lax.dynamic_slice_in_dim(grad_heads, start, block, 0)
        seg_block = lax.dynamic_slice_in_dim(segment_ids, start, block, 0)
        pos_block = start + jnp.arange(block, dtype=jnp.int32)
        allowed = (positions[None, :] <= pos_block[:, None]) & (segment_ids[None, :] == seg_block[:, None])
        scores = jnp.einsum('qngd,knd->ngqk', query_block, key_heads) * scale
        scores = jnp.where(allowed, scores, -1e+30)
        top = lax.optimization_barrier(jnp.max(scores, axis=-1))
        weights = jnp.where(allowed, jnp.exp(scores - top[..., None]), 0.0)
        total = lax.optimization_barrier(jnp.sum(weights, axis=-1))
        weights_b = weights.astype(jnp.bfloat16).astype(jnp.float32)
        attended = (jnp.einsum('ngqk,knd->ngqd', weights_b, value_heads) / total[..., None]).astype(jnp.bfloat16)
        log_total = top + jnp.log(total)
        delta = jnp.einsum('qngd,ngqd->ngq', grad_block, attended.astype(jnp.float32))
        probs = jnp.where(allowed, jnp.exp(scores - log_total[..., None]), 0.0)
        dprob = jnp.einsum('qngd,knd->ngqk', grad_block, value_heads)
        dscore = probs * (dprob - delta[..., None])
        dscore_b = dscore.astype(jnp.bfloat16).astype(jnp.float32)
        probs_b = probs.astype(jnp.bfloat16).astype(jnp.float32)
        query_grad = (jnp.einsum('ngqk,knd->qngd', dscore_b, key_heads) * scale).astype(jnp.bfloat16)
        value_part = jnp.einsum('ngqk,qngd->knd', probs_b, grad_block)
        return (value_sum + value_part, query_grad)
    starts = jnp.arange(TOKENS // block, dtype=jnp.int32) * block
    value_grad, query_blocks = lax.scan(step, jnp.zeros((TOKENS, KVH, HD), jnp.float32), starts)
    query_grads = query_blocks.reshape(TOKENS, QH * HD)
    value_b = value_grad.reshape(TOKENS, KVH * HD).astype(jnp.bfloat16)
    weight_grad = jnp.dot(features.T, value_b, preferred_element_type=jnp.float32) * (1.0 / math.sqrt(TOKENS))
    return (query_grads, weight_grad)
```

```python
import math

import jax
import jax.numpy as jnp
from jax import lax
from jax.experimental import pallas as pl
from jax.experimental.pallas import tpu as pltpu
from jax.sharding import Mesh, PartitionSpec as P

HD = 128
GROUP = 4
DIMS = (8, 2, 4, 4, 2)
AXES = ("y", "zh", "x", "zl", "core")
CTX = ("y", "zh", "x")
TP = ("zl", "core")
BLOCK = 128
CHUNK = 256
LOW = -1e30
FLOOR = -1e29
SCALE = HD ** (-0.5)
SCALE2 = SCALE * math.log2(math.e)
NT = (((1,), (1,)), ((), ()))
TN = (((0,), (0,)), ((), ()))


def chunk_scores(j, x, nx, pos_q, start, kv_ref):
    at = pl.ds(pl.multiple_of(j * CHUNK, CHUNK), CHUNK)
    k = kv_ref[at, 0:HD]
    v = kv_ref[at, HD : 2 * HD]
    r = lax.broadcasted_iota(jnp.int32, (CHUNK, 1), 0)
    per = CHUNK // BLOCK
    pos_k = (j * per + r // BLOCK) * (nx * BLOCK) + x * BLOCK + r % BLOCK
    allowed = (pos_k <= pos_q) & (pos_k >= start)
    return at, k, v, allowed


def head_of(q_ref, n):
    nx, rows, _ = q_ref.shape
    q = q_ref[:, :, n * HD : (n + 1) * HD].reshape(nx * rows, HD)
    do = q_ref[:, :, (GROUP + n) * HD : (GROUP + n + 1) * HD].reshape(nx * rows, HD)
    return q, do


def stats_kernel(nx, sc_ref, start_ref, q_ref, kv_ref, out_ref):
    g, low, x = sc_ref[0], sc_ref[1], sc_ref[2]
    span = nx * BLOCK
    pos_q = g * span + lax.broadcasted_iota(jnp.int32, (1, span), 1)
    start = start_ref[...]
    out_ref[0] = jnp.full((GROUP, span), FLOOR, jnp.float32)
    out_ref[1] = jnp.zeros((GROUP, span), jnp.float32)
    out_ref[2] = jnp.zeros((GROUP, span), jnp.float32)
    per = CHUNK // BLOCK

    def body(j, carry):
        _, k, v, allowed = chunk_scores(j, x, nx, pos_q, start, kv_ref)
        for n in range(GROUP):
            q, do = head_of(q_ref, n)
            s = lax.dot_general(k, q, NT, preferred_element_type=jnp.float32) * SCALE2
            s = jnp.where(allowed, s, LOW)
            dp = lax.dot_general(v, do, NT, preferred_element_type=jnp.float32)
            m_old = out_ref[0, n : n + 1, :]
            m = jnp.maximum(m_old, jnp.max(s, axis=0, keepdims=True))
            alpha = jnp.exp2(m_old - m)
            w = jnp.exp2(s - m)
            out_ref[0, n : n + 1, :] = m
            out_ref[1, n : n + 1, :] = out_ref[1, n : n + 1, :] * alpha + jnp.sum(
                w, axis=0, keepdims=True
            )
            out_ref[2, n : n + 1, :] = out_ref[2, n : n + 1, :] * alpha + jnp.sum(
                w * dp, axis=0, keepdims=True
            )
        return carry

    lax.fori_loop(low // per, g // per + 1, body, 0)


def grad_kernel(nx, sc_ref, start_ref, st_ref, q_ref, kv_ref, dq_ref, dv_ref, acc_ref):
    g, low, x = sc_ref[0], sc_ref[1], sc_ref[2]
    span = nx * BLOCK
    pos_q = g * span + lax.broadcasted_iota(jnp.int32, (1, span), 1)
    start = start_ref[...]
    acc_ref[...] = jnp.zeros(acc_ref.shape, jnp.float32)
    dv_ref[...] = jnp.zeros(dv_ref.shape, dv_ref.dtype)
    per = CHUNK // BLOCK
    top = st_ref[0, 0]
    for i in range(1, nx):
        top = jnp.maximum(top, st_ref[i, 0])
    total = jnp.zeros_like(top)
    num = jnp.zeros_like(top)
    for i in range(nx):
        f = jnp.exp2(st_ref[i, 0] - top)
        total = total + st_ref[i, 1] * f
        num = num + st_ref[i, 2] * f
    log_total = top + jnp.log2(total)
    delta = num / total

    def body(j, carry):
        at, k, v, allowed = chunk_scores(j, x, nx, pos_q, start, kv_ref)
        dv = jnp.zeros((CHUNK, HD), jnp.float32)
        for n in range(GROUP):
            q, do = head_of(q_ref, n)
            s = lax.dot_general(k, q, NT, preferred_element_type=jnp.float32) * SCALE2
            s = jnp.where(allowed, s, LOW)
            dp = lax.dot_general(v, do, NT, preferred_element_type=jnp.float32)
            p = jnp.exp2(s - log_total[n : n + 1, :])
            ds = (p * (dp - delta[n : n + 1, :])).astype(jnp.bfloat16)
            dv = dv + jnp.dot(p.astype(jnp.bfloat16), do, preferred_element_type=jnp.float32)
            acc_ref[n] += lax.dot_general(k, ds, TN, preferred_element_type=jnp.float32)
        dv_ref[at, :] = dv.astype(dv_ref.dtype)
        return carry

    lax.fori_loop(low // per, g // per + 1, body, 0)
    for n in range(GROUP):
        dq_ref[:, n * HD : (n + 1) * HD] = (acc_ref[n] * SCALE).T.astype(dq_ref.dtype)


def spread(piece, axes, count):
    copies = jnp.broadcast_to(piece[None], (count,) + piece.shape)
    return lax.all_to_all(copies, axes, split_axis=0, concat_axis=0, tiled=True)


def per_device(queries, keys, values, out_grad, features, segment_ids):
    ny, nzh, nx, nzl, ncore = (lax.axis_size(a) for a in AXES)
    groups, tps = ny * nzh, nzl * ncore
    tokens = segment_ids.shape[0]
    rows = queries.shape[0]
    span = nx * rows
    g = lax.axis_index(("y", "zh"))
    x = lax.axis_index("x")
    t = lax.axis_index(TP)
    bf16, f32 = jnp.bfloat16, jnp.float32

    kv = spread(jnp.concatenate([keys, values], axis=1), ("y", "zh"), groups)
    kv = kv.reshape(groups * rows, 2 * HD)
    qd = spread(jnp.concatenate([queries, out_grad], axis=1), "x", nx)

    seg_q = lax.dynamic_slice_in_dim(segment_ids, g * span, span, 0)
    ids = jnp.arange(16, dtype=jnp.int32)
    firsts = jnp.sum((segment_ids[None, :] < ids[:, None]).astype(jnp.int32), axis=1)
    start = jnp.sum(jnp.where(seg_q[None, :] == ids[:, None], firsts[:, None], 0), axis=0)
    low = start[0] // span
    scalars = jnp.stack([g, low, x]).astype(jnp.int32)
    start = start.reshape(1, span)

    smem = pl.BlockSpec(memory_space=pltpu.SMEM)
    vmem = pl.BlockSpec(memory_space=pltpu.VMEM)
    params = pltpu.CompilerParams(vmem_limit_bytes=48 * 1024 * 1024)
    stats = pl.pallas_call(
        lambda *refs: stats_kernel(nx, *refs),
        out_shape=jax.ShapeDtypeStruct((3, GROUP, span), f32),
        in_specs=[smem, vmem, vmem, vmem],
        out_specs=vmem,
        compiler_params=params,
    )(scalars, start, qd, kv)
    all_stats = spread(stats, "x", nx)
    dq_part, dv_part = pl.pallas_call(
        lambda *refs: grad_kernel(nx, *refs),
        out_shape=(
            jax.ShapeDtypeStruct((span, GROUP * HD), bf16),
            jax.ShapeDtypeStruct((groups * rows, HD), bf16),
        ),
        in_specs=[smem, vmem, vmem, vmem, vmem],
        out_specs=(vmem, vmem),
        scratch_shapes=[pltpu.VMEM((GROUP, HD, span), f32)],
        compiler_params=params,
    )(scalars, start, all_stats, qd, kv)

    dv = lax.all_to_all(
        dv_part.reshape(groups, rows, HD), ("y", "zh"), split_axis=0, concat_axis=0, tiled=True
    )
    value_b = jnp.sum(dv.astype(f32), axis=0).astype(bf16)
    value_all = lax.all_gather(value_b, TP, axis=1, tiled=True)
    share = features.shape[1] // tps
    own = lax.dynamic_slice_in_dim(features, t * share, share, 1)
    term = lax.dot_general(own, value_all, TN, preferred_element_type=f32)
    ctx = groups * nx
    pieces = lax.all_to_all(
        term.astype(bf16).reshape(ctx, share // ctx, value_all.shape[1]),
        CTX, split_axis=0, concat_axis=0, tiled=True,
    )
    summed = (jnp.sum(pieces.astype(f32), axis=0) * (1.0 / math.sqrt(tokens))).astype(bf16)
    weight_grad = spread(summed, CTX, ctx).reshape(share, value_all.shape[1]).astype(f32)

    dq = lax.all_to_all(
        dq_part.reshape(nx, rows, GROUP * HD), "x", split_axis=0, concat_axis=0, tiled=True
    )
    query_grads = jnp.sum(dq.astype(f32), axis=0).astype(bf16)
    return (query_grads, weight_grad)


def solution(mesh):
    fine = Mesh(mesh.devices.reshape(DIMS), AXES)
    split = P(CTX, TP)
    return jax.shard_map(
        per_device,
        mesh=fine,
        in_specs=(split, split, split, split, P(CTX, None), P()),
        out_specs=(split, P(TP, None)),
        check_vma=False,
    )
```

```python
import math

import jax
import jax.numpy as jnp
from jax import lax
from jax.experimental import pallas as pl
from jax.experimental.pallas import tpu as pltpu
from jax.sharding import Mesh, PartitionSpec as P

HD = 128
GROUP = 4
DIMS = (8, 2, 4, 4, 2)
AXES = ("y", "zh", "x", "zl", "core")
CTX = ("y", "zh", "x")
TP = ("zl", "core")
BLOCK = 128
CHUNK = 256
PER = CHUNK // BLOCK
LOW = -1e30
FLOOR = -1e29
SCALE = HD ** (-0.5)
SCALE2 = SCALE * math.log2(math.e)
NT = (((1,), (1,)), ((), ()))
TN = (((0,), (0,)), ((), ()))


def lanes_of(ref_row, places):
    return jnp.concatenate([ref_row[:, pl.ds(p, BLOCK)] for p in places], axis=1)


def places_of(x, nx):
    return [pl.multiple_of(lax.rem(x + nx - d, nx) * BLOCK, BLOCK) for d in range(nx)]


def positions_of(g, x, nx):
    span = nx * BLOCK
    lane = lax.broadcasted_iota(jnp.int32, (1, BLOCK), 1)
    return jnp.concatenate([g * span + p + lane for p in places_of(x, nx)], axis=1)


def chunk_of(j, kv_ref):
    at = pl.ds(pl.multiple_of(j * CHUNK, CHUNK), CHUNK)
    return at, kv_ref[at, 0:HD], kv_ref[at, HD : 2 * HD]


def allowed_in(j, x, nx, pos_q, start):
    r = lax.broadcasted_iota(jnp.int32, (CHUNK, 1), 0)
    pos_k = (j * PER + r // BLOCK) * (nx * BLOCK) + x * BLOCK + r % BLOCK
    return (pos_k <= pos_q) & (pos_k >= start)


def head_of(q_refs, n):
    q = jnp.concatenate([r[:, n * HD : (n + 1) * HD] for r in q_refs], axis=0)
    do = jnp.concatenate([r[:, (GROUP + n) * HD : (GROUP + n + 1) * HD] for r in q_refs], axis=0)
    return q, do


def over_chunks(g, low, high, nx, step):
    width = PER * nx * BLOCK
    first, last = low // width, g // PER
    clear = jnp.minimum((high + width - 1) // width, last)

    def masked(j, carry):
        step(j, True)
        return carry

    def free(j, carry):
        step(j, False)
        return carry

    lax.fori_loop(first, clear, masked, 0)
    lax.fori_loop(clear, last, free, 0)
    step(last, True)


def stats_kernel(nx, sc_ref, start_ref, *refs):
    q_refs, kv_ref, out_ref, st_ref = refs[:nx], refs[nx], refs[-2], refs[-1]
    g, low, high, x = sc_ref[0], sc_ref[1], sc_ref[2], sc_ref[3]
    span = nx * BLOCK
    pos_q = positions_of(g, x, nx)
    start = lanes_of(start_ref, places_of(x, nx))
    st_ref[0] = jnp.full((GROUP, span), FLOOR, jnp.float32)
    st_ref[1] = jnp.zeros((GROUP, span), jnp.float32)
    st_ref[2] = jnp.zeros((GROUP, span), jnp.float32)

    def step(j, masked):
        _, k, v = chunk_of(j, kv_ref)
        if masked:
            allowed = allowed_in(j, x, nx, pos_q, start)
        for n in range(GROUP):
            q, do = head_of(q_refs, n)
            s = lax.dot_general(k, q, NT, preferred_element_type=jnp.float32) * SCALE2
            if masked:
                s = jnp.where(allowed, s, LOW)
            dp = lax.dot_general(v, do, NT, preferred_element_type=jnp.float32)
            m_old = st_ref[0, n : n + 1, :]
            m = jnp.maximum(m_old, jnp.max(s, axis=0, keepdims=True))
            alpha = jnp.exp2(m_old - m)
            w = jnp.exp2(s - m)
            st_ref[0, n : n + 1, :] = m
            st_ref[1, n : n + 1, :] = st_ref[1, n : n + 1, :] * alpha + jnp.sum(
                w, axis=0, keepdims=True
            )
            st_ref[2, n : n + 1, :] = st_ref[2, n : n + 1, :] * alpha + jnp.sum(
                w * dp, axis=0, keepdims=True
            )

    over_chunks(g, low, high, nx, step)
    for d, p in enumerate(places_of(x, nx)):
        for k in range(3):
            out_ref[k, :, pl.ds(p, BLOCK)] = st_ref[k, :, d * BLOCK : (d + 1) * BLOCK]


def grad_kernel(nx, sc_ref, start_ref, st_ref, *refs):
    q_refs, kv_ref = refs[:nx], refs[nx]
    dq_refs, dv_ref, acc_ref = refs[nx + 1 : 2 * nx + 1], refs[2 * nx + 1], refs[2 * nx + 2]
    g, low, high, x = sc_ref[0], sc_ref[1], sc_ref[2], sc_ref[3]
    places = places_of(x, nx)
    pos_q = positions_of(g, x, nx)
    start = lanes_of(start_ref, places)
    acc_ref[...] = jnp.zeros(acc_ref.shape, jnp.float32)
    dv_ref[...] = jnp.zeros(dv_ref.shape, dv_ref.dtype)
    part = [[lanes_of(st_ref.at[i, k], places) for k in range(3)] for i in range(nx)]
    top = part[0][0]
    for i in range(1, nx):
        top = jnp.maximum(top, part[i][0])
    total = jnp.zeros_like(top)
    num = jnp.zeros_like(top)
    for i in range(nx):
        f = jnp.exp2(part[i][0] - top)
        total = total + part[i][1] * f
        num = num + part[i][2] * f
    log_total = top + jnp.log2(total)
    delta = num / total

    def step(j, masked):
        at, k, v = chunk_of(j, kv_ref)
        if masked:
            allowed = allowed_in(j, x, nx, pos_q, start)
        dv = jnp.zeros((CHUNK, HD), jnp.float32)
        for n in range(GROUP):
            q, do = head_of(q_refs, n)
            s = lax.dot_general(k, q, NT, preferred_element_type=jnp.float32) * SCALE2
            if masked:
                s = jnp.where(allowed, s, LOW)
            dp = lax.dot_general(v, do, NT, preferred_element_type=jnp.float32)
            p = jnp.exp2(s - log_total[n : n + 1, :])
            ds = (p * (dp - delta[n : n + 1, :])).astype(jnp.bfloat16)
            dv = dv + jnp.dot(p.astype(jnp.bfloat16), do, preferred_element_type=jnp.float32)
            acc_ref[n] += lax.dot_general(k, ds, TN, preferred_element_type=jnp.float32)
        dv_ref[at, :] = dv.astype(dv_ref.dtype)

    over_chunks(g, low, high, nx, step)
    for n in range(GROUP):
        dq = (acc_ref[n] * SCALE).T.astype(jnp.bfloat16)
        for d in range(nx):
            dq_refs[d][:, n * HD : (n + 1) * HD] = dq[d * BLOCK : (d + 1) * BLOCK]


def regroup_kernel(nx, tps, sc_ref, f_ref, *out_refs):
    x = sc_ref[3]
    share = f_ref.shape[1] // tps
    wide = share // nx
    for d, out_ref in enumerate(out_refs):
        to = lax.rem(x + d, nx) * wide
        for t in range(tps):
            at = pl.multiple_of(t * share + to, wide)
            out_ref[:, t * wide : (t + 1) * wide] = f_ref[:, pl.ds(at, wide)]


def weight_kernel(nx, sc_ref, v_ref, *refs):
    f_refs, out_ref = refs[:nx], refs[nx]
    ny, tps, part, _ = out_ref.shape
    x = sc_ref[3]
    f = jnp.concatenate([r[...] for r in f_refs], axis=0)
    v = jnp.concatenate([v_ref[lax.rem(x + nx - d, nx)] for d in range(nx)], axis=0)
    term = lax.dot_general(v, f, TN, preferred_element_type=jnp.float32).T
    for t in range(tps):
        for y in range(ny):
            at = (t * ny + y) * part
            out_ref[y, t] = term[at : at + part].astype(out_ref.dtype)


def spread(piece, axes, count):
    copies = jnp.broadcast_to(piece[None], (count,) + piece.shape)
    return lax.all_to_all(copies, axes, split_axis=0, concat_axis=0, tiled=True)


def shift(a, axis, by):
    n = lax.axis_size(axis)
    return lax.ppermute(a, axis, [(i, (i + by) % n) for i in range(n)])


def per_device(queries, keys, values, out_grad, features, segment_ids):
    ny, nzh, nx, nzl, ncore = (lax.axis_size(a) for a in AXES)
    groups, tps = ny * nzh, nzl * ncore
    tokens = segment_ids.shape[0]
    rows = queries.shape[0]
    span = nx * rows
    g = lax.axis_index(("y", "zh"))
    x = lax.axis_index("x")
    bf16, f32 = jnp.bfloat16, jnp.float32

    own = jnp.concatenate([queries, out_grad], axis=1)
    qd = [own] + [shift(own, "x", d) for d in range(1, nx)]
    kv = spread(jnp.concatenate([keys, values], axis=1), ("y", "zh"), groups)
    kv = kv.reshape(groups * rows, 2 * HD)

    seg_q = lax.dynamic_slice_in_dim(segment_ids, g * span, span, 0)
    ids = jnp.arange(16, dtype=jnp.int32)
    firsts = jnp.sum((segment_ids[None, :] < ids[:, None]).astype(jnp.int32), axis=1)
    start = jnp.sum(jnp.where(seg_q[None, :] == ids[:, None], firsts[:, None], 0), axis=0)
    scalars = jnp.stack([g, start[0], start[span - 1], x]).astype(jnp.int32)
    start = start.reshape(1, span)

    smem = pl.BlockSpec(memory_space=pltpu.SMEM)
    vmem = pl.BlockSpec(memory_space=pltpu.VMEM)
    params = pltpu.CompilerParams(vmem_limit_bytes=48 * 1024 * 1024)

    wide = features.shape[1] // nx
    mine = pl.pallas_call(
        lambda *refs: regroup_kernel(nx, tps, *refs),
        out_shape=[jax.ShapeDtypeStruct((rows, wide), bf16)] * nx,
        in_specs=[smem, vmem],
        out_specs=[vmem] * nx,
        compiler_params=params,
    )(scalars, features)
    from_x = [mine[0]] + [shift(mine[d], "x", d) for d in range(1, nx)]

    stats = pl.pallas_call(
        lambda *refs: stats_kernel(nx, *refs),
        out_shape=jax.ShapeDtypeStruct((3, GROUP, span), f32),
        in_specs=[smem, vmem] + [vmem] * (nx + 1) + [pl.BlockSpec(memory_space=pl.ANY)] * nx,
        out_specs=vmem,
        scratch_shapes=[pltpu.VMEM((3, GROUP, span), f32)],
        compiler_params=params,
    )(scalars, start, *qd, kv, *from_x)
    all_stats = spread(stats, "x", nx)
    *dq_parts, dv_part = pl.pallas_call(
        lambda *refs: grad_kernel(nx, *refs),
        out_shape=[jax.ShapeDtypeStruct((rows, GROUP * HD), bf16)] * nx
        + [jax.ShapeDtypeStruct((groups * rows, HD), bf16)],
        in_specs=[smem, vmem, vmem] + [vmem] * (nx + 1),
        out_specs=[vmem] * (nx + 1),
        scratch_shapes=[pltpu.VMEM((GROUP, HD, span), f32)],
        compiler_params=params,
    )(scalars, start, all_stats, *qd, kv)

    dv = lax.all_to_all(
        dv_part.reshape(groups, rows, HD), ("y", "zh"), split_axis=0, concat_axis=0, tiled=True
    )
    dq = dq_parts[0].astype(f32)
    for d in range(1, nx):
        dq = dq + shift(dq_parts[d], "x", -d).astype(f32)
    query_grads = dq.astype(bf16)

    value_b = jnp.sum(dv.astype(f32), axis=0).astype(bf16)
    value_x = spread(value_b, "x", nx)
    part = wide // (tps * ny)
    term = pl.pallas_call(
        lambda *refs: weight_kernel(nx, *refs),
        out_shape=jax.ShapeDtypeStruct((ny, tps, part, HD), bf16),
        in_specs=[smem] + [vmem] * (nx + 1),
        out_specs=vmem,
        compiler_params=params,
    )(scalars, value_x, *from_x)
    pieces = lax.all_to_all(term, "y", split_axis=0, concat_axis=0, tiled=True)
    summed = jnp.sum(pieces.astype(f32), axis=0).astype(bf16)
    turned = lax.all_to_all(
        jnp.broadcast_to(summed[None], (nzh,) + summed.shape).reshape(nzh * tps, part, HD),
        ("zh",) + TP, split_axis=0, concat_axis=0, tiled=True,
    ).reshape(nzh, tps, part, HD)
    own_rows = jnp.sum(turned.astype(f32), axis=0) * (1.0 / math.sqrt(tokens))
    own_rows = own_rows.astype(bf16).transpose(1, 0, 2).reshape(part, tps * HD)
    weight_grad = spread(own_rows, ("x", "y"), nx * ny)
    return (query_grads, weight_grad.reshape(wide // tps * nx, tps * HD).astype(f32))


def solution(mesh):
    fine = Mesh(mesh.devices.reshape(DIMS), AXES)
    split = P(CTX, TP)
    return jax.shard_map(
        per_device,
        mesh=fine,
        in_specs=(split, split, split, split, P(CTX, None), P()),
        out_specs=(split, P(TP, None)),
        check_vma=False,
    )
```

```python
import math

import jax
import jax.numpy as jnp
from jax import lax
from jax.experimental import pallas as pl
from jax.experimental.pallas import tpu as pltpu
from jax.sharding import Mesh, PartitionSpec as P

HD = 128
GROUP = 4
DIMS = (8, 2, 4, 4, 2)
AXES = ("y", "zh", "x", "zl", "core")
CTX = ("y", "zh", "x")
TP = ("zl", "core")
BLOCK = 128
CHUNK = 256
PER = CHUNK // BLOCK
LOW = -1e30
FLOOR = -1e29
SCALE = HD ** (-0.5)
SCALE2 = SCALE * math.log2(math.e)
NT = (((1,), (1,)), ((), ()))
TN = (((0,), (0,)), ((), ()))


def lanes_of(ref_row, places):
    return jnp.concatenate([ref_row[:, pl.ds(p, BLOCK)] for p in places], axis=1)


def places_of(x, nx):
    return [pl.multiple_of(lax.rem(x + nx - d, nx) * BLOCK, BLOCK) for d in range(nx)]


def positions_of(g, x, nx):
    span = nx * BLOCK
    lane = lax.broadcasted_iota(jnp.int32, (1, BLOCK), 1)
    return jnp.concatenate([g * span + p + lane for p in places_of(x, nx)], axis=1)


def chunk_of(j, kv_ref):
    at = pl.ds(pl.multiple_of(j * CHUNK, CHUNK), CHUNK)
    return at, kv_ref[at, 0:HD], kv_ref[at, HD : 2 * HD]


def allowed_in(j, x, nx, pos_q, start):
    r = lax.broadcasted_iota(jnp.int32, (CHUNK, 1), 0)
    pos_k = (j * PER + r // BLOCK) * (nx * BLOCK) + x * BLOCK + r % BLOCK
    return (pos_k <= pos_q) & (pos_k >= start)


def head_of(q_refs, n):
    q = jnp.concatenate([r[:, n * HD : (n + 1) * HD] for r in q_refs], axis=0)
    do = jnp.concatenate([r[:, (GROUP + n) * HD : (GROUP + n + 1) * HD] for r in q_refs], axis=0)
    return q, do


def over_chunks(g, low, high, nx, step):
    width = PER * nx * BLOCK
    first, last = low // width, g // PER
    clear = jnp.minimum((high + width - 1) // width, last)

    def masked(j, carry):
        step(j, True)
        return carry

    def free(j, carry):
        step(j, False)
        return carry

    lax.fori_loop(first, clear, masked, 0)
    lax.fori_loop(clear, last, free, 0)
    step(last, True)


def stats_kernel(nx, sc_ref, start_ref, *refs):
    q_refs, kv_ref, out_ref, st_ref = refs[:nx], refs[nx], refs[-2], refs[-1]
    g, low, high, x = sc_ref[0], sc_ref[1], sc_ref[2], sc_ref[3]
    span = nx * BLOCK
    pos_q = positions_of(g, x, nx)
    start = lanes_of(start_ref, places_of(x, nx))
    st_ref[0] = jnp.full((GROUP, span), FLOOR, jnp.float32)
    st_ref[1] = jnp.zeros((GROUP, span), jnp.float32)
    st_ref[2] = jnp.zeros((GROUP, span), jnp.float32)

    def step(j, masked):
        _, k, v = chunk_of(j, kv_ref)
        if masked:
            allowed = allowed_in(j, x, nx, pos_q, start)
        for n in range(GROUP):
            q, do = head_of(q_refs, n)
            s = lax.dot_general(k, q, NT, preferred_element_type=jnp.float32) * SCALE2
            if masked:
                s = jnp.where(allowed, s, LOW)
            dp = lax.dot_general(v, do, NT, preferred_element_type=jnp.float32)
            m_old = st_ref[0, n : n + 1, :]
            m = jnp.maximum(m_old, jnp.max(s, axis=0, keepdims=True))
            alpha = jnp.exp2(m_old - m)
            w = jnp.exp2(s - m)
            st_ref[0, n : n + 1, :] = m
            st_ref[1, n : n + 1, :] = st_ref[1, n : n + 1, :] * alpha + jnp.sum(
                w, axis=0, keepdims=True
            )
            st_ref[2, n : n + 1, :] = st_ref[2, n : n + 1, :] * alpha + jnp.sum(
                w * dp, axis=0, keepdims=True
            )

    over_chunks(g, low, high, nx, step)
    for d, p in enumerate(places_of(x, nx)):
        for k in range(3):
            for i in range(nx):
                out_ref[i, k, :, pl.ds(p, BLOCK)] = st_ref[k, :, d * BLOCK : (d + 1) * BLOCK]


def grad_kernel(nx, sc_ref, start_ref, st_ref, *refs):
    q_refs, kv_ref = refs[:nx], refs[nx]
    dq_refs, dv_ref, acc_ref = refs[nx + 1 : 2 * nx + 1], refs[2 * nx + 1], refs[2 * nx + 2]
    g, low, high, x = sc_ref[0], sc_ref[1], sc_ref[2], sc_ref[3]
    places = places_of(x, nx)
    pos_q = positions_of(g, x, nx)
    start = lanes_of(start_ref, places)
    acc_ref[...] = jnp.zeros(acc_ref.shape, jnp.float32)
    dv_ref[...] = jnp.zeros(dv_ref.shape, dv_ref.dtype)
    part = [[lanes_of(st_ref.at[i, k], places) for k in range(3)] for i in range(nx)]
    top = part[0][0]
    for i in range(1, nx):
        top = jnp.maximum(top, part[i][0])
    total = jnp.zeros_like(top)
    num = jnp.zeros_like(top)
    for i in range(nx):
        f = jnp.exp2(part[i][0] - top)
        total = total + part[i][1] * f
        num = num + part[i][2] * f
    log_total = top + jnp.log2(total)
    delta = num / total

    def step(j, masked):
        at, k, v = chunk_of(j, kv_ref)
        if masked:
            allowed = allowed_in(j, x, nx, pos_q, start)
        dv = jnp.zeros((CHUNK, HD), jnp.float32)
        for n in range(GROUP):
            q, do = head_of(q_refs, n)
            s = lax.dot_general(k, q, NT, preferred_element_type=jnp.float32) * SCALE2
            if masked:
                s = jnp.where(allowed, s, LOW)
            dp = lax.dot_general(v, do, NT, preferred_element_type=jnp.float32)
            p = jnp.exp2(s - log_total[n : n + 1, :])
            ds = (p * (dp - delta[n : n + 1, :])).astype(jnp.bfloat16)
            dv = dv + jnp.dot(p.astype(jnp.bfloat16), do, preferred_element_type=jnp.float32)
            acc_ref[n] += lax.dot_general(k, ds, TN, preferred_element_type=jnp.float32)
        dv_ref[at, :] = dv.astype(dv_ref.dtype)

    over_chunks(g, low, high, nx, step)
    for n in range(GROUP):
        dq = (acc_ref[n] * SCALE).T.astype(jnp.bfloat16)
        for d in range(nx):
            dq_refs[d][:, n * HD : (n + 1) * HD] = dq[d * BLOCK : (d + 1) * BLOCK]


def regroup_kernel(nx, tps, sc_ref, f_ref, _, *out_refs):
    x = sc_ref[3]
    share = f_ref.shape[1] // tps
    wide = share // nx
    for d, out_ref in enumerate(out_refs):
        to = lax.rem(x + d, nx) * wide
        for t in range(tps):
            at = pl.multiple_of(t * share + to, wide)
            out_ref[:, t * wide : (t + 1) * wide] = f_ref[:, pl.ds(at, wide)]


def weight_kernel(nx, sc_ref, v_ref, *refs):
    f_refs, out_ref = refs[:nx], refs[nx]
    ny, tps, part, _ = out_ref.shape
    x = sc_ref[3]
    f = jnp.concatenate([r[...] for r in f_refs], axis=0)
    v = jnp.concatenate([v_ref[lax.rem(x + nx - d, nx)] for d in range(nx)], axis=0)
    term = lax.dot_general(v, f, TN, preferred_element_type=jnp.float32).T
    for t in range(tps):
        for y in range(ny):
            at = (t * ny + y) * part
            out_ref[y, t] = term[at : at + part].astype(out_ref.dtype)


def pair_kernel(k_ref, v_ref, out_ref):
    for i in range(out_ref.shape[0]):
        out_ref[i, :, 0:HD] = k_ref[...]
        out_ref[i, :, HD : 2 * HD] = v_ref[...]


def sum_kernel(in_ref, *refs):
    out_ref = refs[-1]
    total = in_ref[0].astype(jnp.float32)
    for i in range(1, in_ref.shape[0]):
        total = total + in_ref[i].astype(jnp.float32)
    total = total.astype(out_ref.dtype)
    for i in range(out_ref.shape[0]):
        out_ref[i] = total


def turn_kernel(nzh, factor, in_ref, out_ref):
    tps = in_ref.shape[0] // nzh
    parts = []
    for t in range(tps):
        total = in_ref[t].astype(jnp.float32)
        for i in range(1, nzh):
            total = total + in_ref[i * tps + t].astype(jnp.float32)
        parts.append((total * factor).astype(out_ref.dtype))
    whole = jnp.concatenate(parts, axis=1)
    for i in range(out_ref.shape[0]):
        out_ref[i] = whole


def shift(a, axis, by):
    n = lax.axis_size(axis)
    return lax.ppermute(a, axis, [(i, (i + by) % n) for i in range(n)])


def per_device(queries, keys, values, out_grad, features, segment_ids):
    ny, nzh, nx, nzl, ncore = (lax.axis_size(a) for a in AXES)
    groups, tps = ny * nzh, nzl * ncore
    tokens = segment_ids.shape[0]
    rows = queries.shape[0]
    span = nx * rows
    g = lax.axis_index(("y", "zh"))
    x = lax.axis_index("x")
    bf16, f32 = jnp.bfloat16, jnp.float32

    smem = pl.BlockSpec(memory_space=pltpu.SMEM)
    vmem = pl.BlockSpec(memory_space=pltpu.VMEM)
    unread = pl.BlockSpec(memory_space=pl.ANY)
    params = pltpu.CompilerParams(vmem_limit_bytes=20 * 1024 * 1024)

    own = jnp.concatenate([queries, out_grad], axis=1)
    qd = [own] + [shift(own, "x", d) for d in range(1, nx)]
    kv_copies = pl.pallas_call(
        pair_kernel,
        out_shape=jax.ShapeDtypeStruct((groups, rows, 2 * HD), bf16),
        in_specs=[vmem, vmem],
        out_specs=vmem,
        compiler_params=params,
    )(keys, values)
    kv = lax.all_to_all(kv_copies, ("y", "zh"), split_axis=0, concat_axis=0, tiled=True)
    kv = kv.reshape(groups * rows, 2 * HD)

    seg_q = lax.dynamic_slice_in_dim(segment_ids, g * span, span, 0)
    ids = jnp.arange(16, dtype=jnp.int32)
    firsts = jnp.sum((segment_ids[None, :] < ids[:, None]).astype(jnp.int32), axis=1)
    start = jnp.sum(jnp.where(seg_q[None, :] == ids[:, None], firsts[:, None], 0), axis=0)
    scalars = jnp.stack([g, start[0], start[span - 1], x]).astype(jnp.int32)
    start = start.reshape(1, span)

    stats = pl.pallas_call(
        lambda *refs: stats_kernel(nx, *refs),
        out_shape=jax.ShapeDtypeStruct((nx, 3, GROUP, span), f32),
        in_specs=[smem, vmem] + [vmem] * (nx + 1),
        out_specs=vmem,
        scratch_shapes=[pltpu.VMEM((3, GROUP, span), f32)],
        compiler_params=params,
    )(scalars, start, *qd, kv)
    all_stats = lax.all_to_all(stats, "x", split_axis=0, concat_axis=0, tiled=True)
    *dq_parts, dv_part = pl.pallas_call(
        lambda *refs: grad_kernel(nx, *refs),
        out_shape=[jax.ShapeDtypeStruct((rows, GROUP * HD), bf16)] * nx
        + [jax.ShapeDtypeStruct((groups * rows, HD), bf16)],
        in_specs=[smem, vmem, vmem] + [vmem] * (nx + 1),
        out_specs=[vmem] * (nx + 1),
        scratch_shapes=[pltpu.VMEM((GROUP, HD, span), f32)],
        compiler_params=params,
    )(scalars, start, all_stats, *qd, kv)

    dv = lax.all_to_all(
        dv_part.reshape(groups, rows, HD), ("y", "zh"), split_axis=0, concat_axis=0, tiled=True
    )
    wide = features.shape[1] // nx
    mine = pl.pallas_call(
        lambda *refs: regroup_kernel(nx, tps, *refs),
        out_shape=[jax.ShapeDtypeStruct((rows, wide), bf16)] * nx,
        in_specs=[smem, vmem, unread],
        out_specs=[vmem] * nx,
        compiler_params=params,
    )(scalars, features, dv_part)
    from_x = [mine[0]] + [shift(mine[d], "x", d) for d in range(1, nx)]
    value_copies = pl.pallas_call(
        sum_kernel,
        out_shape=jax.ShapeDtypeStruct((nx, rows, HD), bf16),
        in_specs=[vmem] + [unread] * nx,
        out_specs=vmem,
        compiler_params=params,
    )(dv, *from_x)
    value_x = lax.all_to_all(value_copies, "x", split_axis=0, concat_axis=0, tiled=True)
    part = wide // (tps * ny)
    term = pl.pallas_call(
        lambda *refs: weight_kernel(nx, *refs),
        out_shape=jax.ShapeDtypeStruct((ny, tps, part, HD), bf16),
        in_specs=[smem] + [vmem] * (nx + 1),
        out_specs=vmem,
        compiler_params=params,
    )(scalars, value_x, *from_x)
    pieces = lax.all_to_all(term, "y", split_axis=0, concat_axis=0, tiled=True)
    row_copies = pl.pallas_call(
        sum_kernel,
        out_shape=jax.ShapeDtypeStruct((nzh, tps, part, HD), bf16),
        in_specs=[vmem],
        out_specs=vmem,
        compiler_params=params,
    )(pieces)
    turned = lax.all_to_all(
        row_copies.reshape(nzh * tps, part, HD),
        ("zh",) + TP, split_axis=0, concat_axis=0, tiled=True,
    )
    final_copies = pl.pallas_call(
        lambda *refs: turn_kernel(nzh, 1.0 / math.sqrt(tokens), *refs),
        out_shape=jax.ShapeDtypeStruct((nx * ny, part, tps * HD), bf16),
        in_specs=[vmem],
        out_specs=vmem,
        compiler_params=params,
    )(turned)
    weight_grad = lax.all_to_all(final_copies, ("x", "y"), split_axis=0, concat_axis=0, tiled=True)

    dq = dq_parts[0].astype(f32)
    for d in range(1, nx):
        dq = dq + shift(dq_parts[d], "x", -d).astype(f32)
    query_grads = dq.astype(bf16)
    return (query_grads, weight_grad.reshape(wide // tps * nx, tps * HD).astype(f32))


def solution(mesh):
    fine = Mesh(mesh.devices.reshape(DIMS), AXES)
    split = P(CTX, TP)
    return jax.shard_map(
        per_device,
        mesh=fine,
        in_specs=(split, split, split, split, P(CTX, None), P()),
        out_specs=(split, P(TP, None)),
        check_vma=False,
    )
```

```python
import math

import jax
import jax.numpy as jnp
from jax import lax
from jax.experimental import pallas as pl
from jax.experimental.pallas import tpu as pltpu
from jax.sharding import Mesh, PartitionSpec as P

HD = 128
GROUP = 4
DIMS = (4, 2, 2, 4, 4, 2)
AXES = ("yh", "yl", "zh", "x", "zl", "core")
CTX = ("yh", "yl", "zh", "x")
Y = ("yh", "yl")
TP = ("zl", "core")
QUERY = ("yl", "x")
KEY = ("yh", "zh")
BLOCK = 128
LOW = -1e30
FLOOR = -1e29
SCALE = HD ** (-0.5)
SCALE2 = SCALE * math.log2(math.e)
NT = (((1,), (1,)), ((), ()))
TN = (((0,), (0,)), ((), ()))


class Place:
    def __init__(self, sizes, sc_ref):
        self.nyl, self.nzh, self.nx = sizes
        self.yh, self.yl, self.zh, self.x, self.low, self.high = (sc_ref[i] for i in range(6))
        self.pieces = self.nyl * self.nx
        self.run = self.nx * BLOCK
        self.step = self.nyl * self.nzh * self.run
        self.width = self.pieces * BLOCK
        self.origin = [
            (lax.rem(self.yl + self.nyl - e, self.nyl), lax.rem(self.x + self.nx - d, self.nx))
            for e in range(self.nyl)
            for d in range(self.nx)
        ]
        self.lanes = [pl.multiple_of((yl * self.nx + x) * BLOCK, BLOCK) for yl, x in self.origin]

    def gather(self, row_ref):
        return jnp.concatenate([row_ref[:, pl.ds(at, BLOCK)] for at in self.lanes], axis=1)

    def queries(self):
        lane = lax.broadcasted_iota(jnp.int32, (1, BLOCK), 1)
        base = self.yh * self.step + self.zh * self.run
        return jnp.concatenate(
            [base + yl * self.nzh * self.run + x * BLOCK + lane for yl, x in self.origin], axis=1
        )

    def chunk(self):
        return self.nzh * BLOCK

    def keys(self, j):
        r = lax.broadcasted_iota(jnp.int32, (self.chunk(), 1), 0)
        base = j * self.step + self.yl * self.nzh * self.run + self.x * BLOCK
        return base + (r // BLOCK) * self.run + r % BLOCK

    def over_chunks(self, step):
        first, last = self.low // self.step, self.yh
        clear = jnp.minimum((self.high + self.step - 1) // self.step, last)

        def masked(j, carry):
            step(j, True)
            return carry

        def free(j, carry):
            step(j, False)
            return carry

        lax.fori_loop(first, clear, masked, 0)
        lax.fori_loop(clear, last, free, 0)
        step(last, True)


def chunk_of(j, size, kv_ref):
    at = pl.ds(pl.multiple_of(j * size, size), size)
    return at, kv_ref[at, 0:HD], kv_ref[at, HD : 2 * HD]


def head_of(q_refs, n):
    q = jnp.concatenate([r[:, n * HD : (n + 1) * HD] for r in q_refs], axis=0)
    do = jnp.concatenate([r[:, (GROUP + n) * HD : (GROUP + n + 1) * HD] for r in q_refs], axis=0)
    return q, do


def stats_kernel(sizes, sc_ref, start_ref, *refs):
    place = Place(sizes, sc_ref)
    count, span = place.pieces, place.width
    q_refs, kv_ref, out_ref, st_ref = refs[:count], refs[count], refs[-2], refs[-1]
    pos_q, start = place.queries(), place.gather(start_ref)
    st_ref[0] = jnp.full((GROUP, span), FLOOR, jnp.float32)
    st_ref[1] = jnp.zeros((GROUP, span), jnp.float32)
    st_ref[2] = jnp.zeros((GROUP, span), jnp.float32)

    def step(j, masked):
        _, k, v = chunk_of(j, place.chunk(), kv_ref)
        if masked:
            pos_k = place.keys(j)
            allowed = (pos_k <= pos_q) & (pos_k >= start)
        for n in range(GROUP):
            q, do = head_of(q_refs, n)
            s = lax.dot_general(k, q, NT, preferred_element_type=jnp.float32) * SCALE2
            if masked:
                s = jnp.where(allowed, s, LOW)
            dp = lax.dot_general(v, do, NT, preferred_element_type=jnp.float32)
            m_old = st_ref[0, n : n + 1, :]
            m = jnp.maximum(m_old, jnp.max(s, axis=0, keepdims=True))
            alpha = jnp.exp2(m_old - m)
            w = jnp.exp2(s - m)
            st_ref[0, n : n + 1, :] = m
            st_ref[1, n : n + 1, :] = st_ref[1, n : n + 1, :] * alpha + jnp.sum(
                w, axis=0, keepdims=True
            )
            st_ref[2, n : n + 1, :] = st_ref[2, n : n + 1, :] * alpha + jnp.sum(
                w * dp, axis=0, keepdims=True
            )

    place.over_chunks(step)
    for i, at in enumerate(place.lanes):
        for k in range(3):
            row = st_ref[k, :, i * BLOCK : (i + 1) * BLOCK]
            for copy in range(count):
                out_ref[copy, k, :, pl.ds(at, BLOCK)] = row


def grad_kernel(sizes, sc_ref, start_ref, st_ref, *refs):
    place = Place(sizes, sc_ref)
    count, span = place.pieces, place.width
    q_refs, kv_ref, (*dq_refs, dv_ref, acc_ref) = refs[:count], refs[count], refs[count + 1 :]
    pos_q, start = place.queries(), place.gather(start_ref)
    acc_ref[...] = jnp.zeros(acc_ref.shape, jnp.float32)
    dv_ref[...] = jnp.zeros(dv_ref.shape, dv_ref.dtype)
    part = [[place.gather(st_ref.at[i, k]) for k in range(3)] for i in range(count)]
    top = part[0][0]
    for i in range(1, count):
        top = jnp.maximum(top, part[i][0])
    total = jnp.zeros_like(top)
    num = jnp.zeros_like(top)
    for i in range(count):
        f = jnp.exp2(part[i][0] - top)
        total = total + part[i][1] * f
        num = num + part[i][2] * f
    log_total = top + jnp.log2(total)
    delta = num / total

    def step(j, masked):
        at, k, v = chunk_of(j, place.chunk(), kv_ref)
        if masked:
            pos_k = place.keys(j)
            allowed = (pos_k <= pos_q) & (pos_k >= start)
        dv = jnp.zeros((place.chunk(), HD), jnp.float32)
        for n in range(GROUP):
            q, do = head_of(q_refs, n)
            s = lax.dot_general(k, q, NT, preferred_element_type=jnp.float32) * SCALE2
            if masked:
                s = jnp.where(allowed, s, LOW)
            dp = lax.dot_general(v, do, NT, preferred_element_type=jnp.float32)
            p = jnp.exp2(s - log_total[n : n + 1, :])
            ds = (p * (dp - delta[n : n + 1, :])).astype(jnp.bfloat16)
            dv = dv + jnp.dot(p.astype(jnp.bfloat16), do, preferred_element_type=jnp.float32)
            acc_ref[n] += lax.dot_general(k, ds, TN, preferred_element_type=jnp.float32)
        dv_ref[at, :] = dv.astype(dv_ref.dtype)

    place.over_chunks(step)
    nx = place.nx
    for n in range(GROUP):
        dq = (acc_ref[n] * SCALE).T.astype(jnp.bfloat16)
        for i in range(count):
            dq_refs[i % nx][i // nx, :, n * HD : (n + 1) * HD] = dq[i * BLOCK : (i + 1) * BLOCK]


def join_kernel(*refs):
    *in_refs, away_ref, own_ref = refs
    total = in_refs[0][...].astype(jnp.float32)
    for r in in_refs[1:]:
        total = total + r[...].astype(jnp.float32)
    own_ref[...] = total[0]
    away_ref[...] = total[1].astype(away_ref.dtype)


def regroup_kernel(nx, tps, sc_ref, f_ref, _, *out_refs):
    x = sc_ref[3]
    share = f_ref.shape[1] // tps
    wide = share // nx
    for d, out_ref in enumerate(out_refs):
        to = lax.rem(x + d, nx) * wide
        for t in range(tps):
            at = pl.multiple_of(t * share + to, wide)
            out_ref[:, t * wide : (t + 1) * wide] = f_ref[:, pl.ds(at, wide)]


def weight_kernel(nx, sc_ref, v_ref, *refs):
    f_refs, out_ref = refs[:nx], refs[nx]
    ny, tps, part, _ = out_ref.shape
    x = sc_ref[3]
    f = jnp.concatenate([r[...] for r in f_refs], axis=0)
    v = jnp.concatenate([v_ref[lax.rem(x + nx - d, nx)] for d in range(nx)], axis=0)
    term = lax.dot_general(v, f, TN, preferred_element_type=jnp.float32).T
    for t in range(tps):
        for y in range(ny):
            at = (t * ny + y) * part
            out_ref[y, t] = term[at : at + part].astype(out_ref.dtype)


def sum_kernel(in_ref, *refs):
    out_ref = refs[-1]
    total = in_ref[0].astype(jnp.float32)
    for i in range(1, in_ref.shape[0]):
        total = total + in_ref[i].astype(jnp.float32)
    total = total.astype(out_ref.dtype)
    for i in range(out_ref.shape[0]):
        out_ref[i] = total


def turn_kernel(nzh, factor, in_ref, _, out_ref):
    tps = in_ref.shape[0] // nzh
    parts = []
    for t in range(tps):
        total = in_ref[t].astype(jnp.float32)
        for i in range(1, nzh):
            total = total + in_ref[i * tps + t].astype(jnp.float32)
        parts.append((total * factor).astype(out_ref.dtype))
    whole = jnp.concatenate(parts, axis=1)
    for i in range(out_ref.shape[0]):
        out_ref[i] = whole


def shift(a, axis, by):
    n = lax.axis_size(axis)
    return lax.ppermute(a, axis, [(i, (i + by) % n) for i in range(n)])


def per_device(queries, keys, values, out_grad, features, segment_ids):
    nyh, nyl, nzh, nx, nzl, ncore = (lax.axis_size(a) for a in AXES)
    ny, tps = nyh * nyl, nzl * ncore
    sizes = (nyl, nzh, nx)
    tokens = segment_ids.shape[0]
    rows = queries.shape[0]
    bf16, f32 = jnp.bfloat16, jnp.float32
    smem = pl.BlockSpec(memory_space=pltpu.SMEM)
    vmem = pl.BlockSpec(memory_space=pltpu.VMEM)
    unread = pl.BlockSpec(memory_space=pl.ANY)
    params = pltpu.CompilerParams(vmem_limit_bytes=24 * 1024 * 1024)

    kv_copies = jnp.broadcast_to(
        jnp.concatenate([keys, values], axis=1)[None], (nyh * nzh, rows, 2 * HD)
    )
    kv = lax.all_to_all(kv_copies, KEY, split_axis=0, concat_axis=0, tiled=True)
    kv = kv.reshape(nyh * nzh * rows, 2 * HD)
    own = jnp.concatenate([queries, out_grad], axis=1)
    pieces = [own] + [shift(own, "yl", e) for e in range(1, nyl)]
    qd = [shift(p, "x", d) if d else p for p in pieces for d in range(nx)]

    yh, yl, zh, x = (lax.axis_index(a) for a in CTX)
    base = (yh * nyl * nzh + zh) * nx * rows
    seg_q = jnp.concatenate(
        [
            lax.dynamic_slice_in_dim(segment_ids, base + i * nzh * nx * rows, nx * rows, 0)
            for i in range(nyl)
        ]
    )
    ids = jnp.arange(16, dtype=jnp.int32)
    firsts = jnp.sum((segment_ids[None, :] < ids[:, None]).astype(jnp.int32), axis=1)
    start = jnp.sum(jnp.where(seg_q[None, :] == ids[:, None], firsts[:, None], 0), axis=0)
    scalars = jnp.stack([yh, yl, zh, x, start[0], start[-1]]).astype(jnp.int32)
    start = start.reshape(1, nyl * nx * rows)

    count = nyl * nx
    stats = pl.pallas_call(
        lambda *refs: stats_kernel(sizes, *refs),
        out_shape=jax.ShapeDtypeStruct((count, 3, GROUP, count * rows), f32),
        in_specs=[smem, vmem] + [vmem] * (count + 1),
        out_specs=vmem,
        scratch_shapes=[pltpu.VMEM((3, GROUP, count * rows), f32)],
        compiler_params=params,
    )(scalars, start, *qd, kv)
    all_stats = lax.all_to_all(stats, QUERY, split_axis=0, concat_axis=0, tiled=True)
    *dq_parts, dv_part = pl.pallas_call(
        lambda *refs: grad_kernel(sizes, *refs),
        out_shape=[jax.ShapeDtypeStruct((nyl, rows, GROUP * HD), bf16)] * nx
        + [jax.ShapeDtypeStruct((nyh * nzh * rows, HD), bf16)],
        in_specs=[smem, vmem, vmem] + [vmem] * (count + 1),
        out_specs=[vmem] * (nx + 1),
        scratch_shapes=[pltpu.VMEM((GROUP, HD, count * rows), f32)],
        compiler_params=params,
    )(scalars, start, all_stats, *qd, kv)

    dv = lax.all_to_all(
        dv_part.reshape(nyh * nzh, rows, HD), KEY, split_axis=0, concat_axis=0, tiled=True
    )
    wide = features.shape[1] // nx
    mine = pl.pallas_call(
        lambda *refs: regroup_kernel(nx, tps, *refs),
        out_shape=[jax.ShapeDtypeStruct((rows, wide), bf16)] * nx,
        in_specs=[smem, vmem, unread],
        out_specs=[vmem] * nx,
        compiler_params=params,
    )(scalars, features, stats)
    from_x = [mine[0]] + [shift(mine[d], "x", d) for d in range(1, nx)]
    value_copies = pl.pallas_call(
        sum_kernel,
        out_shape=jax.ShapeDtypeStruct((nx, rows, HD), bf16),
        in_specs=[vmem] + [unread] * (nx - 1),
        out_specs=vmem,
        compiler_params=params,
    )(dv, *from_x[1:])
    value_x = lax.all_to_all(value_copies, "x", split_axis=0, concat_axis=0, tiled=True)
    part = wide // (tps * ny)
    term = pl.pallas_call(
        lambda *refs: weight_kernel(nx, *refs),
        out_shape=jax.ShapeDtypeStruct((ny, tps, part, HD), bf16),
        in_specs=[smem] + [vmem] * (nx + 1),
        out_specs=vmem,
        compiler_params=params,
    )(scalars, value_x, *from_x)
    pieces = lax.all_to_all(term, Y, split_axis=0, concat_axis=0, tiled=True)

    dq_x = [dq_parts[0]] + [shift(dq_parts[d], "x", -d) for d in range(1, nx)]
    away, at_home = pl.pallas_call(
        join_kernel,
        out_shape=(
            jax.ShapeDtypeStruct((rows, GROUP * HD), bf16),
            jax.ShapeDtypeStruct((rows, GROUP * HD), f32),
        ),
        in_specs=[vmem] * nx,
        out_specs=(vmem, vmem),
        compiler_params=params,
    )(*dq_x)

    row_copies = pl.pallas_call(
        sum_kernel,
        out_shape=jax.ShapeDtypeStruct((nzh, tps, part, HD), bf16),
        in_specs=[vmem],
        out_specs=vmem,
        compiler_params=params,
    )(pieces)
    turned = lax.all_to_all(
        row_copies.reshape(nzh * tps, part, HD),
        ("zh",) + TP, split_axis=0, concat_axis=0, tiled=True,
    )
    final_copies = pl.pallas_call(
        lambda *refs: turn_kernel(nzh, 1.0 / math.sqrt(tokens), *refs),
        out_shape=jax.ShapeDtypeStruct((nx * ny, part, tps * HD), bf16),
        in_specs=[vmem, unread],
        out_specs=vmem,
        compiler_params=params,
    )(turned, away)
    weight_grad = lax.all_to_all(
        final_copies, ("x",) + Y, split_axis=0, concat_axis=0, tiled=True
    )
    query_grads = (at_home + shift(away, "yl", 1).astype(f32)).astype(bf16)
    return (query_grads, weight_grad.reshape(wide // tps * nx, tps * HD).astype(f32))


def solution(mesh):
    fine = Mesh(mesh.devices.reshape(DIMS), AXES)
    split = P(CTX, TP)
    return jax.shard_map(
        per_device,
        mesh=fine,
        in_specs=(split, split, split, split, P(CTX, None), P()),
        out_specs=(split, P(TP, None)),
        check_vma=False,
    )
```

```python
import math

import jax
import jax.numpy as jnp
from jax import lax
from jax.experimental import pallas as pl
from jax.experimental.pallas import tpu as pltpu
from jax.sharding import Mesh, PartitionSpec as P

HD = 128
GROUP = 4
DIMS = (8, 2, 4, 4, 2)
AXES = ("y", "zh", "x", "zl", "core")
CTX = ("y", "zh", "x")
TP = ("zl", "core")
BLOCK = 128
CHUNK = 256
PER = CHUNK // BLOCK
LOW = -1e30
FLOOR = -1e29
SCALE = HD ** (-0.5)
SCALE2 = SCALE * math.log2(math.e)
NT = (((1,), (1,)), ((), ()))
TN = (((0,), (0,)), ((), ()))


def lanes_of(ref_row, places):
    return jnp.concatenate([ref_row[:, pl.ds(p, BLOCK)] for p in places], axis=1)


def places_of(x, nx):
    return [pl.multiple_of(lax.rem(x + nx - d, nx) * BLOCK, BLOCK) for d in range(nx)]


def positions_of(g, x, nx):
    span = nx * BLOCK
    lane = lax.broadcasted_iota(jnp.int32, (1, BLOCK), 1)
    return jnp.concatenate([g * span + p + lane for p in places_of(x, nx)], axis=1)


def chunk_of(j, kv_ref):
    at = pl.ds(pl.multiple_of(j * CHUNK, CHUNK), CHUNK)
    return at, kv_ref[at, 0:HD], kv_ref[at, HD : 2 * HD]


def allowed_in(j, x, nx, pos_q, start):
    r = lax.broadcasted_iota(jnp.int32, (CHUNK, 1), 0)
    pos_k = (j * PER + r // BLOCK) * (nx * BLOCK) + x * BLOCK + r % BLOCK
    return (pos_k <= pos_q) & (pos_k >= start)


def head_of(q_refs, n):
    q = jnp.concatenate([r[:, n * HD : (n + 1) * HD] for r in q_refs], axis=0)
    do = jnp.concatenate([r[:, (GROUP + n) * HD : (GROUP + n + 1) * HD] for r in q_refs], axis=0)
    return q, do


def over_chunks(g, low, high, nx, step):
    width = PER * nx * BLOCK
    first, last = low // width, g // PER
    clear = jnp.minimum((high + width - 1) // width, last)

    def masked(j, carry):
        step(j, True)
        return carry

    def free(j, carry):
        step(j, False)
        return carry

    lax.fori_loop(first, clear, masked, 0)
    lax.fori_loop(clear, last, free, 0)
    step(last, True)


def stats_kernel(nx, sc_ref, start_ref, *refs):
    q_refs, kv_ref, out_ref, st_ref = refs[:nx], refs[nx], refs[-2], refs[-1]
    g, low, high, x = sc_ref[0], sc_ref[1], sc_ref[2], sc_ref[3]
    span = nx * BLOCK
    pos_q = positions_of(g, x, nx)
    start = lanes_of(start_ref, places_of(x, nx))
    st_ref[0] = jnp.full((GROUP, span), FLOOR, jnp.float32)
    st_ref[1] = jnp.zeros((GROUP, span), jnp.float32)
    st_ref[2] = jnp.zeros((GROUP, span), jnp.float32)

    def step(j, masked):
        _, k, v = chunk_of(j, kv_ref)
        if masked:
            allowed = allowed_in(j, x, nx, pos_q, start)
        for n in range(GROUP):
            q, do = head_of(q_refs, n)
            s = lax.dot_general(k, q, NT, preferred_element_type=jnp.float32) * SCALE2
            if masked:
                s = jnp.where(allowed, s, LOW)
            dp = lax.dot_general(v, do, NT, preferred_element_type=jnp.float32)
            m_old = st_ref[0, n : n + 1, :]
            m = jnp.maximum(m_old, jnp.max(s, axis=0, keepdims=True))
            alpha = jnp.exp2(m_old - m)
            w = jnp.exp2(s - m)
            st_ref[0, n : n + 1, :] = m
            st_ref[1, n : n + 1, :] = st_ref[1, n : n + 1, :] * alpha + jnp.sum(
                w, axis=0, keepdims=True
            )
            st_ref[2, n : n + 1, :] = st_ref[2, n : n + 1, :] * alpha + jnp.sum(
                w * dp, axis=0, keepdims=True
            )

    over_chunks(g, low, high, nx, step)
    for d, p in enumerate(places_of(x, nx)):
        for k in range(3):
            out_ref[k, :, pl.ds(p, BLOCK)] = st_ref[k, :, d * BLOCK : (d + 1) * BLOCK]


def combined(st_ref, places):
    nx = len(places)
    part = [[lanes_of(st_ref.at[i, k], places) for k in range(3)] for i in range(nx)]
    top = part[0][0]
    for i in range(1, nx):
        top = jnp.maximum(top, part[i][0])
    total = jnp.zeros_like(top)
    num = jnp.zeros_like(top)
    for i in range(nx):
        f = jnp.exp2(part[i][0] - top)
        total = total + part[i][1] * f
        num = num + part[i][2] * f
    return top + jnp.log2(total), num / total


def value_kernel(nx, sc_ref, start_ref, st_ref, *refs):
    q_refs, kv_ref, dv_ref = refs[:nx], refs[nx], refs[nx + 1]
    g, low, high, x = sc_ref[0], sc_ref[1], sc_ref[2], sc_ref[3]
    places = places_of(x, nx)
    pos_q = positions_of(g, x, nx)
    start = lanes_of(start_ref, places)
    dv_ref[...] = jnp.zeros(dv_ref.shape, dv_ref.dtype)
    log_total, _ = combined(st_ref, places)

    def step(j, masked):
        at, k, _ = chunk_of(j, kv_ref)
        if masked:
            allowed = allowed_in(j, x, nx, pos_q, start)
        dv = jnp.zeros((CHUNK, HD), jnp.float32)
        for n in range(GROUP):
            q, do = head_of(q_refs, n)
            s = lax.dot_general(k, q, NT, preferred_element_type=jnp.float32) * SCALE2
            if masked:
                s = jnp.where(allowed, s, LOW)
            p = jnp.exp2(s - log_total[n : n + 1, :])
            dv = dv + jnp.dot(p.astype(jnp.bfloat16), do, preferred_element_type=jnp.float32)
        dv_ref[at, :] = dv.astype(dv_ref.dtype)

    over_chunks(g, low, high, nx, step)


def query_kernel(nx, sc_ref, start_ref, st_ref, *refs):
    q_refs, kv_ref, (*dq_refs, done_ref, acc_ref) = refs[:nx], refs[nx], refs[nx + 2 :]
    done_ref[...] = jnp.zeros(done_ref.shape, done_ref.dtype)
    g, low, high, x = sc_ref[0], sc_ref[1], sc_ref[2], sc_ref[3]
    places = places_of(x, nx)
    pos_q = positions_of(g, x, nx)
    start = lanes_of(start_ref, places)
    acc_ref[...] = jnp.zeros(acc_ref.shape, jnp.float32)
    log_total, delta = combined(st_ref, places)

    def step(j, masked):
        _, k, v = chunk_of(j, kv_ref)
        if masked:
            allowed = allowed_in(j, x, nx, pos_q, start)
        for n in range(GROUP):
            q, do = head_of(q_refs, n)
            s = lax.dot_general(k, q, NT, preferred_element_type=jnp.float32) * SCALE2
            if masked:
                s = jnp.where(allowed, s, LOW)
            dp = lax.dot_general(v, do, NT, preferred_element_type=jnp.float32)
            p = jnp.exp2(s - log_total[n : n + 1, :])
            ds = (p * (dp - delta[n : n + 1, :])).astype(jnp.bfloat16)
            acc_ref[n] += lax.dot_general(k, ds, TN, preferred_element_type=jnp.float32)

    over_chunks(g, low, high, nx, step)
    for n in range(GROUP):
        dq = (acc_ref[n] * SCALE).T.astype(jnp.bfloat16)
        for d in range(nx):
            dq_refs[d][:, n * HD : (n + 1) * HD] = dq[d * BLOCK : (d + 1) * BLOCK]


def regroup_kernel(nx, tps, sc_ref, f_ref, *out_refs):
    x = sc_ref[3]
    share = f_ref.shape[1] // tps
    wide = share // nx
    for d, out_ref in enumerate(out_refs):
        to = lax.rem(x + d, nx) * wide
        for t in range(tps):
            at = pl.multiple_of(t * share + to, wide)
            out_ref[:, t * wide : (t + 1) * wide] = f_ref[:, pl.ds(at, wide)]


def sum_kernel(in_ref, *refs):
    out_ref = refs[-1]
    total = in_ref[0].astype(jnp.float32)
    for i in range(1, in_ref.shape[0]):
        total = total + in_ref[i].astype(jnp.float32)
    total = total.astype(out_ref.dtype)
    for i in range(out_ref.shape[0]):
        out_ref[i] = total


def weight_kernel(nx, sc_ref, v_ref, *refs):
    f_refs, out_ref = refs[:nx], refs[nx]
    ny, tps, part, _ = out_ref.shape
    x = sc_ref[3]
    f = jnp.concatenate([r[...] for r in f_refs], axis=0)
    v = jnp.concatenate([v_ref[lax.rem(x + nx - d, nx)] for d in range(nx)], axis=0)
    term = lax.dot_general(v, f, TN, preferred_element_type=jnp.float32).T
    for t in range(tps):
        for y in range(ny):
            at = (t * ny + y) * part
            out_ref[y, t] = term[at : at + part].astype(out_ref.dtype)


def spread(piece, axes, count):
    copies = jnp.broadcast_to(piece[None], (count,) + piece.shape)
    return lax.all_to_all(copies, axes, split_axis=0, concat_axis=0, tiled=True)


def shift(a, axis, by):
    n = lax.axis_size(axis)
    return lax.ppermute(a, axis, [(i, (i + by) % n) for i in range(n)])


def per_device(queries, keys, values, out_grad, features, segment_ids):
    ny, nzh, nx, nzl, ncore = (lax.axis_size(a) for a in AXES)
    groups, tps = ny * nzh, nzl * ncore
    tokens = segment_ids.shape[0]
    rows = queries.shape[0]
    span = nx * rows
    g = lax.axis_index(("y", "zh"))
    x = lax.axis_index("x")
    bf16, f32 = jnp.bfloat16, jnp.float32

    own = jnp.concatenate([queries, out_grad], axis=1)
    qd = [own] + [shift(own, "x", d) for d in range(1, nx)]
    kv = spread(jnp.concatenate([keys, values], axis=1), ("y", "zh"), groups)
    kv = kv.reshape(groups * rows, 2 * HD)

    seg_q = lax.dynamic_slice_in_dim(segment_ids, g * span, span, 0)
    ids = jnp.arange(16, dtype=jnp.int32)
    firsts = jnp.sum((segment_ids[None, :] < ids[:, None]).astype(jnp.int32), axis=1)
    start = jnp.sum(jnp.where(seg_q[None, :] == ids[:, None], firsts[:, None], 0), axis=0)
    scalars = jnp.stack([g, start[0], start[span - 1], x]).astype(jnp.int32)
    start = start.reshape(1, span)

    smem = pl.BlockSpec(memory_space=pltpu.SMEM)
    vmem = pl.BlockSpec(memory_space=pltpu.VMEM)
    unread = pl.BlockSpec(memory_space=pl.ANY)
    params = pltpu.CompilerParams(vmem_limit_bytes=24 * 1024 * 1024)

    wide = features.shape[1] // nx
    mine = pl.pallas_call(
        lambda *refs: regroup_kernel(nx, tps, *refs),
        out_shape=[jax.ShapeDtypeStruct((rows, wide), bf16)] * nx,
        in_specs=[smem, vmem],
        out_specs=[vmem] * nx,
        compiler_params=params,
    )(scalars, features)
    from_x = [mine[0]] + [shift(mine[d], "x", d) for d in range(1, nx)]

    stats = pl.pallas_call(
        lambda *refs: stats_kernel(nx, *refs),
        out_shape=jax.ShapeDtypeStruct((3, GROUP, span), f32),
        in_specs=[smem, vmem] + [vmem] * (nx + 1) + [unread] * (nx - 1),
        out_specs=vmem,
        scratch_shapes=[pltpu.VMEM((3, GROUP, span), f32)],
        compiler_params=params,
    )(scalars, start, *qd, kv, *from_x[1:])
    all_stats = spread(stats, "x", nx)
    dv_part = pl.pallas_call(
        lambda *refs: value_kernel(nx, *refs),
        out_shape=jax.ShapeDtypeStruct((groups * rows, HD), bf16),
        in_specs=[smem, vmem, vmem] + [vmem] * (nx + 1),
        out_specs=vmem,
        compiler_params=params,
    )(scalars, start, all_stats, *qd, kv)
    *dq_parts, done = pl.pallas_call(
        lambda *refs: query_kernel(nx, *refs),
        out_shape=[jax.ShapeDtypeStruct((rows, GROUP * HD), bf16)] * nx
        + [jax.ShapeDtypeStruct((8, BLOCK), f32)],
        in_specs=[smem, vmem, vmem] + [vmem] * (nx + 1) + [unread],
        out_specs=[vmem] * (nx + 1),
        scratch_shapes=[pltpu.VMEM((GROUP, HD, span), f32)],
        compiler_params=params,
    )(scalars, start, all_stats, *qd, kv, dv_part)

    dv = lax.all_to_all(
        dv_part.reshape(groups, rows, HD), ("y", "zh"), split_axis=0, concat_axis=0, tiled=True
    )
    value_copies = pl.pallas_call(
        sum_kernel,
        out_shape=jax.ShapeDtypeStruct((nx, rows, HD), bf16),
        in_specs=[vmem, vmem],
        out_specs=vmem,
        compiler_params=params,
    )(dv, done)
    value_x = lax.all_to_all(value_copies, "x", split_axis=0, concat_axis=0, tiled=True)
    part = wide // (tps * ny)
    term = pl.pallas_call(
        lambda *refs: weight_kernel(nx, *refs),
        out_shape=jax.ShapeDtypeStruct((ny, tps, part, HD), bf16),
        in_specs=[smem] + [vmem] * (nx + 1),
        out_specs=vmem,
        compiler_params=params,
    )(scalars, value_x, *from_x)
    pieces = lax.all_to_all(term, "y", split_axis=0, concat_axis=0, tiled=True)
    summed = jnp.sum(pieces.astype(f32), axis=0).astype(bf16)
    turned = lax.all_to_all(
        jnp.broadcast_to(summed[None], (nzh,) + summed.shape).reshape(nzh * tps, part, HD),
        ("zh",) + TP, split_axis=0, concat_axis=0, tiled=True,
    ).reshape(nzh, tps, part, HD)
    own_rows = jnp.sum(turned.astype(f32), axis=0) * (1.0 / math.sqrt(tokens))
    own_rows = own_rows.astype(bf16).transpose(1, 0, 2).reshape(part, tps * HD)
    weight_grad = spread(own_rows, ("x", "y"), nx * ny)
    dq = dq_parts[0].astype(f32)
    for d in range(1, nx):
        dq = dq + shift(dq_parts[d], "x", -d).astype(f32)
    query_grads = dq.astype(bf16)
    return (query_grads, weight_grad.reshape(wide // tps * nx, tps * HD).astype(f32))


def solution(mesh):
    fine = Mesh(mesh.devices.reshape(DIMS), AXES)
    split = P(CTX, TP)
    return jax.shard_map(
        per_device,
        mesh=fine,
        in_specs=(split, split, split, split, P(CTX, None), P()),
        out_specs=(split, P(TP, None)),
        check_vma=False,
    )
```

```python
import math

import jax
import jax.numpy as jnp
from jax import lax
from jax.experimental import pallas as pl
from jax.experimental.pallas import tpu as pltpu
from jax.sharding import Mesh, PartitionSpec as P

HD = 128
GROUP = 4
DIMS = (8, 2, 4, 4, 2)
AXES = ("y", "zh", "x", "zl", "core")
CTX = ("y", "zh", "x")
TP = ("zl", "core")
BLOCK = 128
VM = 16
CHUNK = 256
PER = CHUNK // BLOCK
LOW = -1e30
FLOOR = -1e29
SCALE = HD ** (-0.5)
SCALE2 = SCALE * math.log2(math.e)
NT = (((1,), (1,)), ((), ()))
TN = (((0,), (0,)), ((), ()))


def lanes_of(ref_row, places):
    return jnp.concatenate([ref_row[:, pl.ds(p, BLOCK)] for p in places], axis=1)


def places_of(x, nx):
    return [pl.multiple_of(lax.rem(x + nx - d, nx) * BLOCK, BLOCK) for d in range(nx)]


def positions_of(g, x, nx):
    span = nx * BLOCK
    lane = lax.broadcasted_iota(jnp.int32, (1, BLOCK), 1)
    return jnp.concatenate([g * span + p + lane for p in places_of(x, nx)], axis=1)


def chunk_of(j, wide, kv_ref):
    at = pl.ds(pl.multiple_of(j * CHUNK, CHUNK), wide * CHUNK)
    return at, kv_ref[at, 0:HD], kv_ref[at, HD : 2 * HD]


def allowed_in(j, x, nx, pos_q, start):
    r = lax.broadcasted_iota(jnp.int32, (CHUNK, 1), 0)
    pos_k = (j * PER + r // BLOCK) * (nx * BLOCK) + x * BLOCK + r % BLOCK
    return (pos_k <= pos_q) & (pos_k >= start)


def head_of(q_refs, n):
    q = jnp.concatenate([r[:, n * HD : (n + 1) * HD] for r in q_refs], axis=0)
    do = jnp.concatenate([r[:, (GROUP + n) * HD : (GROUP + n + 1) * HD] for r in q_refs], axis=0)
    return q, do


def over_chunks(g, low, high, nx, step):
    width = PER * nx * BLOCK
    first, last = low // width, g // PER
    clear = jnp.minimum((high + width - 1) // width, last)
    pairs = (last - clear) // 2

    def masked(j, carry):
        step(j, 1, True)
        return carry

    def pair(i, carry):
        step(clear + 2 * i, 2, False)
        return carry

    def single(j, carry):
        step(j, 1, False)
        return carry

    lax.fori_loop(first, clear, masked, 0)
    lax.fori_loop(0, pairs, pair, 0)
    lax.fori_loop(clear + 2 * pairs, last, single, 0)
    step(last, 1, True)


def stats_kernel(nx, sc_ref, start_ref, *refs):
    q_refs, kv_ref, out_ref, st_ref = refs[:nx], refs[nx], refs[-2], refs[-1]
    g, low, high, x = sc_ref[0], sc_ref[1], sc_ref[2], sc_ref[3]
    span = nx * BLOCK
    pos_q = positions_of(g, x, nx)
    start = lanes_of(start_ref, places_of(x, nx))
    st_ref[0] = jnp.full((GROUP, span), FLOOR, jnp.float32)
    st_ref[1] = jnp.zeros((GROUP, span), jnp.float32)
    st_ref[2] = jnp.zeros((GROUP, span), jnp.float32)

    def step(j, wide, masked):
        _, k, v = chunk_of(j, wide, kv_ref)
        if masked:
            allowed = allowed_in(j, x, nx, pos_q, start)
        old = [[st_ref[k, n : n + 1, :] for k in range(3)] for n in range(GROUP)]
        new = []
        for n in range(GROUP):
            q, do = head_of(q_refs, n)
            s = lax.dot_general(k, q, NT, preferred_element_type=jnp.float32) * SCALE2
            if masked:
                s = jnp.where(allowed, s, LOW)
            dp = lax.dot_general(v, do, NT, preferred_element_type=jnp.float32)
            m_old, l_old, d_old = old[n]
            m = jnp.maximum(m_old, jnp.max(s, axis=0, keepdims=True))
            alpha = jnp.exp2(m_old - m)
            w = jnp.exp2(s - m)
            l = l_old * alpha + jnp.sum(w, axis=0, keepdims=True)
            new.append((m, l, d_old * alpha + jnp.sum(w * dp, axis=0, keepdims=True)))
        for n in range(GROUP):
            for k in range(3):
                st_ref[k, n : n + 1, :] = new[n][k]

    over_chunks(g, low, high, nx, step)
    for d, p in enumerate(places_of(x, nx)):
        for k in range(3):
            out_ref[k, :, pl.ds(p, BLOCK)] = st_ref[k, :, d * BLOCK : (d + 1) * BLOCK]


def combined(st_ref, places):
    nx = len(places)
    part = [[lanes_of(st_ref.at[i, k], places) for k in range(3)] for i in range(nx)]
    top = part[0][0]
    for i in range(1, nx):
        top = jnp.maximum(top, part[i][0])
    total = jnp.zeros_like(top)
    num = jnp.zeros_like(top)
    for i in range(nx):
        f = jnp.exp2(part[i][0] - top)
        total = total + part[i][1] * f
        num = num + part[i][2] * f
    return top + jnp.log2(total), num / total


def value_kernel(nx, sc_ref, start_ref, st_ref, *refs):
    q_refs, kv_ref, dv_ref = refs[:nx], refs[nx], refs[nx + 1]
    g, low, high, x = sc_ref[0], sc_ref[1], sc_ref[2], sc_ref[3]
    places = places_of(x, nx)
    pos_q = positions_of(g, x, nx)
    start = lanes_of(start_ref, places)
    dv_ref[...] = jnp.zeros(dv_ref.shape, dv_ref.dtype)
    log_total, _ = combined(st_ref, places)

    def step(j, wide, masked):
        at, k, _ = chunk_of(j, wide, kv_ref)
        if masked:
            allowed = allowed_in(j, x, nx, pos_q, start)
        heads = [head_of(q_refs, n) for n in range(GROUP)]
        ps = []
        for n in range(GROUP):
            s = lax.dot_general(k, heads[n][0], NT, preferred_element_type=jnp.float32) * SCALE2
            if masked:
                s = jnp.where(allowed, s, LOW)
            ps.append(jnp.exp2(s - log_total[n : n + 1, :]).astype(jnp.bfloat16))
        dv = jnp.dot(
            jnp.concatenate(ps, axis=1),
            jnp.concatenate([do for _, do in heads], axis=0),
            preferred_element_type=jnp.float32,
        )
        dv_ref[at, :] = dv.astype(dv_ref.dtype)

    over_chunks(g, low, high, nx, step)


def query_kernel(nx, sc_ref, start_ref, st_ref, *refs):
    q_refs, kv_ref, (*dq_refs, done_ref, acc_ref) = refs[:nx], refs[nx], refs[nx + 2 :]
    done_ref[...] = jnp.zeros(done_ref.shape, done_ref.dtype)
    g, low, high, x = sc_ref[0], sc_ref[1], sc_ref[2], sc_ref[3]
    places = places_of(x, nx)
    pos_q = positions_of(g, x, nx)
    start = lanes_of(start_ref, places)
    acc_ref[...] = jnp.zeros(acc_ref.shape, jnp.float32)
    log_total, delta = combined(st_ref, places)

    def step(j, wide, masked):
        _, k, v = chunk_of(j, wide, kv_ref)
        if masked:
            allowed = allowed_in(j, x, nx, pos_q, start)
        for n in range(GROUP):
            q, do = head_of(q_refs, n)
            s = lax.dot_general(k, q, NT, preferred_element_type=jnp.float32) * SCALE2
            if masked:
                s = jnp.where(allowed, s, LOW)
            dp = lax.dot_general(v, do, NT, preferred_element_type=jnp.float32)
            p = jnp.exp2(s - log_total[n : n + 1, :])
            ds = (p * (dp - delta[n : n + 1, :])).astype(jnp.bfloat16)
            acc_ref[n] += lax.dot_general(k, ds, TN, preferred_element_type=jnp.float32)

    over_chunks(g, low, high, nx, step)
    for n in range(GROUP):
        dq = (acc_ref[n] * SCALE).T.astype(jnp.bfloat16)
        for d in range(nx):
            dq_refs[d][:, n * HD : (n + 1) * HD] = dq[d * BLOCK : (d + 1) * BLOCK]


def regroup_kernel(nx, tps, sc_ref, f_ref, *out_refs):
    x = sc_ref[3]
    share = f_ref.shape[1] // tps
    wide = share // nx
    for d, out_ref in enumerate(out_refs):
        to = lax.rem(x + d, nx) * wide
        for t in range(tps):
            at = pl.multiple_of(t * share + to, wide)
            out_ref[:, t * wide : (t + 1) * wide] = f_ref[:, pl.ds(at, wide)]


def sum_kernel(in_ref, *refs):
    out_ref = refs[-1]
    total = in_ref[0].astype(jnp.float32)
    for i in range(1, in_ref.shape[0]):
        total = total + in_ref[i].astype(jnp.float32)
    total = total.astype(out_ref.dtype)
    for i in range(out_ref.shape[0]):
        out_ref[i] = total


def weight_kernel(nx, sc_ref, v_ref, *refs):
    f_refs, out_ref = refs[:nx], refs[nx]
    ny, tps, part, _ = out_ref.shape
    x = sc_ref[3]
    f = jnp.concatenate([r[...] for r in f_refs], axis=0)
    v = jnp.concatenate([v_ref[lax.rem(x + nx - d, nx)] for d in range(nx)], axis=0)
    term = lax.dot_general(v, f, TN, preferred_element_type=jnp.float32).T
    for t in range(tps):
        for y in range(ny):
            at = (t * ny + y) * part
            out_ref[y, t] = term[at : at + part].astype(out_ref.dtype)


def spread(piece, axes, count):
    copies = jnp.broadcast_to(piece[None], (count,) + piece.shape)
    return lax.all_to_all(copies, axes, split_axis=0, concat_axis=0, tiled=True)


def shift(a, axis, by):
    n = lax.axis_size(axis)
    return lax.ppermute(a, axis, [(i, (i + by) % n) for i in range(n)])


def per_device(queries, keys, values, out_grad, features, segment_ids):
    ny, nzh, nx, nzl, ncore = (lax.axis_size(a) for a in AXES)
    groups, tps = ny * nzh, nzl * ncore
    tokens = segment_ids.shape[0]
    rows = queries.shape[0]
    span = nx * rows
    g = lax.axis_index(("y", "zh"))
    x = lax.axis_index("x")
    bf16, f32 = jnp.bfloat16, jnp.float32

    own = jnp.concatenate([queries, out_grad], axis=1)
    qd = [own] + [shift(own, "x", d) for d in range(1, nx)]
    kv = spread(jnp.concatenate([keys, values], axis=1), ("y", "zh"), groups)
    kv = kv.reshape(groups * rows, 2 * HD)

    seg_q = lax.dynamic_slice_in_dim(segment_ids, g * span, span, 0)
    ids = jnp.arange(16, dtype=jnp.int32)
    firsts = jnp.sum((segment_ids[None, :] < ids[:, None]).astype(jnp.int32), axis=1)
    start = jnp.sum(jnp.where(seg_q[None, :] == ids[:, None], firsts[:, None], 0), axis=0)
    scalars = jnp.stack([g, start[0], start[span - 1], x]).astype(jnp.int32)
    start = start.reshape(1, span)

    smem = pl.BlockSpec(memory_space=pltpu.SMEM)
    vmem = pl.BlockSpec(memory_space=pltpu.VMEM)
    unread = pl.BlockSpec(memory_space=pl.ANY)
    params = pltpu.CompilerParams(vmem_limit_bytes=VM * 1024 * 1024)

    wide = features.shape[1] // nx
    mine = pl.pallas_call(
        lambda *refs: regroup_kernel(nx, tps, *refs),
        out_shape=[jax.ShapeDtypeStruct((rows, wide), bf16)] * nx,
        in_specs=[smem, vmem],
        out_specs=[vmem] * nx,
        compiler_params=params,
    )(scalars, features)
    from_x = [mine[0]] + [shift(mine[d], "x", d) for d in range(1, nx)]

    stats = pl.pallas_call(
        lambda *refs: stats_kernel(nx, *refs),
        out_shape=jax.ShapeDtypeStruct((3, GROUP, span), f32),
        in_specs=[smem, vmem] + [vmem] * (nx + 1) + [unread] * (nx - 1),
        out_specs=vmem,
        scratch_shapes=[pltpu.VMEM((3, GROUP, span), f32)],
        compiler_params=params,
    )(scalars, start, *qd, kv, *from_x[1:])
    all_stats = spread(stats, "x", nx)
    dv_part = pl.pallas_call(
        lambda *refs: value_kernel(nx, *refs),
        out_shape=jax.ShapeDtypeStruct((groups * rows, HD), bf16),
        in_specs=[smem, vmem, vmem] + [vmem] * (nx + 1),
        out_specs=vmem,
        compiler_params=params,
    )(scalars, start, all_stats, *qd, kv)
    *dq_parts, done = pl.pallas_call(
        lambda *refs: query_kernel(nx, *refs),
        out_shape=[jax.ShapeDtypeStruct((rows, GROUP * HD), bf16)] * nx
        + [jax.ShapeDtypeStruct((8, BLOCK), f32)],
        in_specs=[smem, vmem, vmem] + [vmem] * (nx + 1) + [unread],
        out_specs=[vmem] * (nx + 1),
        scratch_shapes=[pltpu.VMEM((GROUP, HD, span), f32)],
        compiler_params=params,
    )(scalars, start, all_stats, *qd, kv, dv_part)

    dv = lax.all_to_all(
        dv_part.reshape(groups, rows, HD), ("y", "zh"), split_axis=0, concat_axis=0, tiled=True
    )
    value_copies = pl.pallas_call(
        sum_kernel,
        out_shape=jax.ShapeDtypeStruct((nx, rows, HD), bf16),
        in_specs=[vmem, vmem],
        out_specs=vmem,
        compiler_params=params,
    )(dv, done)
    value_x = lax.all_to_all(value_copies, "x", split_axis=0, concat_axis=0, tiled=True)
    part = wide // (tps * ny)
    term = pl.pallas_call(
        lambda *refs: weight_kernel(nx, *refs),
        out_shape=jax.ShapeDtypeStruct((ny, tps, part, HD), bf16),
        in_specs=[smem] + [vmem] * (nx + 1),
        out_specs=vmem,
        compiler_params=params,
    )(scalars, value_x, *from_x)
    pieces = lax.all_to_all(term, "y", split_axis=0, concat_axis=0, tiled=True)
    summed = jnp.sum(pieces.astype(f32), axis=0).astype(bf16)
    turned = lax.all_to_all(
        jnp.broadcast_to(summed[None], (nzh,) + summed.shape).reshape(nzh * tps, part, HD),
        ("zh",) + TP, split_axis=0, concat_axis=0, tiled=True,
    ).reshape(nzh, tps, part, HD)
    own_rows = jnp.sum(turned.astype(f32), axis=0) * (1.0 / math.sqrt(tokens))
    own_rows = own_rows.astype(bf16).transpose(1, 0, 2).reshape(part, tps * HD)
    weight_grad = spread(own_rows, ("x", "y"), nx * ny)
    dq = dq_parts[0].astype(f32)
    for d in range(1, nx):
        dq = dq + shift(dq_parts[d], "x", -d).astype(f32)
    query_grads = dq.astype(bf16)
    return (query_grads, weight_grad.reshape(wide // tps * nx, tps * HD).astype(f32))


def solution(mesh):
    fine = Mesh(mesh.devices.reshape(DIMS), AXES)
    split = P(CTX, TP)
    return jax.shard_map(
        per_device,
        mesh=fine,
        in_specs=(split, split, split, split, P(CTX, None), P()),
        out_specs=(split, P(TP, None)),
        check_vma=False,
    )
```

```python
import math

import jax
import jax.numpy as jnp
from jax import lax
from jax.experimental import pallas as pl
from jax.experimental.pallas import tpu as pltpu
from jax.sharding import Mesh, PartitionSpec as P

HD = 128
GROUP = 4
DIMS = (8, 2, 4, 4, 2)
AXES = ("y", "zh", "x", "zl", "core")
CTX = ("y", "zh", "x")
TP = ("zl", "core")
BLOCK = 128
VM = 16
CHUNK = 256
PER = CHUNK // BLOCK
LOW = -1e30
FLOOR = -1e29
SCALE = HD ** (-0.5)
SCALE2 = SCALE * math.log2(math.e)
NT = (((1,), (1,)), ((), ()))
TN = (((0,), (0,)), ((), ()))


def lanes_of(ref_row, places):
    return jnp.concatenate([ref_row[:, pl.ds(p, BLOCK)] for p in places], axis=1)


def places_of(x, nx):
    return [pl.multiple_of(lax.rem(x + nx - d, nx) * BLOCK, BLOCK) for d in range(nx)]


def positions_of(g, x, nx):
    span = nx * BLOCK
    lane = lax.broadcasted_iota(jnp.int32, (1, BLOCK), 1)
    return jnp.concatenate([g * span + p + lane for p in places_of(x, nx)], axis=1)


def chunk_of(j, wide, kv_ref):
    at = pl.ds(pl.multiple_of(j * CHUNK, CHUNK), wide * CHUNK)
    return at, kv_ref[at, 0:HD], kv_ref[at, HD : 2 * HD]


def allowed_in(j, x, nx, pos_q, start):
    r = lax.broadcasted_iota(jnp.int32, (CHUNK, 1), 0)
    pos_k = (j * PER + r // BLOCK) * (nx * BLOCK) + x * BLOCK + r % BLOCK
    return (pos_k <= pos_q) & (pos_k >= start)


def head_of(q_refs, n):
    q = jnp.concatenate([r[:, n * HD : (n + 1) * HD] for r in q_refs], axis=0)
    do = jnp.concatenate([r[:, (GROUP + n) * HD : (GROUP + n + 1) * HD] for r in q_refs], axis=0)
    return q, do


def over_chunks(g, low, high, nx, step):
    width = PER * nx * BLOCK
    first, last = low // width, g // PER
    clear = jnp.minimum((high + width - 1) // width, last)
    pairs = (last - clear) // 2

    def masked(j, carry):
        step(j, 1, True)
        return carry

    def pair(i, carry):
        step(clear + 2 * i, 2, False)
        return carry

    def single(j, carry):
        step(j, 1, False)
        return carry

    lax.fori_loop(first, clear, masked, 0)
    lax.fori_loop(0, pairs, pair, 0)
    lax.fori_loop(clear + 2 * pairs, last, single, 0)
    step(last, 1, True)


def stats_kernel(nx, sc_ref, start_ref, *refs):
    q_refs, kv_ref, out_ref, st_ref = refs[:nx], refs[nx], refs[-2], refs[-1]
    g, low, high, x = sc_ref[0], sc_ref[1], sc_ref[2], sc_ref[3]
    span = nx * BLOCK
    pos_q = positions_of(g, x, nx)
    start = lanes_of(start_ref, places_of(x, nx))
    st_ref[0] = jnp.full((GROUP, span), FLOOR, jnp.float32)
    st_ref[1] = jnp.zeros((GROUP, span), jnp.float32)
    st_ref[2] = jnp.zeros((GROUP, span), jnp.float32)

    def step(j, wide, masked):
        _, k, v = chunk_of(j, wide, kv_ref)
        if masked:
            allowed = allowed_in(j, x, nx, pos_q, start)
        old = [[st_ref[k, n : n + 1, :] for k in range(3)] for n in range(GROUP)]
        new = []
        for n in range(GROUP):
            q, do = head_of(q_refs, n)
            s = lax.dot_general(k, q, NT, preferred_element_type=jnp.float32) * SCALE2
            if masked:
                s = jnp.where(allowed, s, LOW)
            dp = lax.dot_general(v, do, NT, preferred_element_type=jnp.float32)
            m_old, l_old, d_old = old[n]
            m = jnp.maximum(m_old, jnp.max(s, axis=0, keepdims=True))
            alpha = jnp.exp2(m_old - m)
            w = jnp.exp2(s - m)
            l = l_old * alpha + jnp.sum(w, axis=0, keepdims=True)
            new.append((m, l, d_old * alpha + jnp.sum(w * dp, axis=0, keepdims=True)))
        for n in range(GROUP):
            for k in range(3):
                st_ref[k, n : n + 1, :] = new[n][k]

    over_chunks(g, low, high, nx, step)
    for d, p in enumerate(places_of(x, nx)):
        for k in range(3):
            out_ref[k, :, pl.ds(p, BLOCK)] = st_ref[k, :, d * BLOCK : (d + 1) * BLOCK]


def combined(st_ref, places):
    nx = len(places)
    part = [[lanes_of(st_ref.at[i, k], places) for k in range(3)] for i in range(nx)]
    top = part[0][0]
    for i in range(1, nx):
        top = jnp.maximum(top, part[i][0])
    total = jnp.zeros_like(top)
    num = jnp.zeros_like(top)
    for i in range(nx):
        f = jnp.exp2(part[i][0] - top)
        total = total + part[i][1] * f
        num = num + part[i][2] * f
    return top + jnp.log2(total), num / total


def value_kernel(nx, sc_ref, start_ref, st_ref, *refs):
    q_refs, kv_ref, dv_ref = refs[:nx], refs[nx], refs[nx + 1]
    g, low, high, x = sc_ref[0], sc_ref[1], sc_ref[2], sc_ref[3]
    places = places_of(x, nx)
    pos_q = positions_of(g, x, nx)
    start = lanes_of(start_ref, places)
    dv_ref[...] = jnp.zeros(dv_ref.shape, dv_ref.dtype)
    log_total, _ = combined(st_ref, places)

    def step(j, wide, masked):
        at, k, _ = chunk_of(j, wide, kv_ref)
        if masked:
            allowed = allowed_in(j, x, nx, pos_q, start)
        heads = [head_of(q_refs, n) for n in range(GROUP)]
        ps = []
        for n in range(GROUP):
            s = lax.dot_general(k, heads[n][0], NT, preferred_element_type=jnp.float32) * SCALE2
            if masked:
                s = jnp.where(allowed, s, LOW)
            ps.append(jnp.exp2(s - log_total[n : n + 1, :]).astype(jnp.bfloat16))
        dv = jnp.dot(
            jnp.concatenate(ps, axis=1),
            jnp.concatenate([do for _, do in heads], axis=0),
            preferred_element_type=jnp.float32,
        )
        dv_ref[at, :] = dv.astype(dv_ref.dtype)

    over_chunks(g, low, high, nx, step)


def query_kernel(nx, heads, sc_ref, start_ref, st_ref, *refs):
    q_refs, kv_ref, acc_ref = refs[:nx], refs[nx], refs[-1]
    g, low, high, x = sc_ref[0], sc_ref[1], sc_ref[2], sc_ref[3]
    places = places_of(x, nx)
    pos_q = positions_of(g, x, nx)
    start = lanes_of(start_ref, places)
    acc_ref[...] = jnp.zeros(acc_ref.shape, jnp.float32)
    log_total, delta = combined(st_ref, places)

    def step(j, wide, masked):
        _, k, v = chunk_of(j, wide, kv_ref)
        if masked:
            allowed = allowed_in(j, x, nx, pos_q, start)
        for i, n in enumerate(heads):
            q, do = head_of(q_refs, n)
            s = lax.dot_general(k, q, NT, preferred_element_type=jnp.float32) * SCALE2
            if masked:
                s = jnp.where(allowed, s, LOW)
            dp = lax.dot_general(v, do, NT, preferred_element_type=jnp.float32)
            p = jnp.exp2(s - log_total[n : n + 1, :])
            ds = (p * (dp - delta[n : n + 1, :])).astype(jnp.bfloat16)
            acc_ref[i] += lax.dot_general(k, ds, TN, preferred_element_type=jnp.float32)

    over_chunks(g, low, high, nx, step)
    return [(acc_ref[i] * SCALE).T.astype(jnp.bfloat16) for i in range(len(heads))]


def first_query_kernel(nx, heads, *refs):
    out_ref = refs[-2]
    for i, dq in enumerate(query_kernel(nx, heads, *refs)):
        for d in range(nx):
            out_ref[d, :, i * HD : (i + 1) * HD] = dq[d * BLOCK : (d + 1) * BLOCK]


def last_query_kernel(nx, heads, *refs):
    before_ref, dq_refs, done_ref = refs[nx + 4], refs[-2 - nx : -2], refs[-2]
    done_ref[...] = jnp.zeros(done_ref.shape, done_ref.dtype)
    wide = before_ref.shape[2]
    for d in range(nx):
        dq_refs[d][:, 0:wide] = before_ref[d]
    for i, dq in enumerate(query_kernel(nx, heads, *refs)):
        for d in range(nx):
            dq_refs[d][:, wide + i * HD : wide + (i + 1) * HD] = dq[d * BLOCK : (d + 1) * BLOCK]


def regroup_kernel(nx, tps, sc_ref, f_ref, *out_refs):
    x = sc_ref[3]
    share = f_ref.shape[1] // tps
    wide = share // nx
    for d, out_ref in enumerate(out_refs):
        to = lax.rem(x + d, nx) * wide
        for t in range(tps):
            at = pl.multiple_of(t * share + to, wide)
            out_ref[:, t * wide : (t + 1) * wide] = f_ref[:, pl.ds(at, wide)]


def sum_kernel(in_ref, *refs):
    out_ref = refs[-1]
    total = in_ref[0].astype(jnp.float32)
    for i in range(1, in_ref.shape[0]):
        total = total + in_ref[i].astype(jnp.float32)
    total = total.astype(out_ref.dtype)
    for i in range(out_ref.shape[0]):
        out_ref[i] = total


def stack_kernel(*refs):
    *in_refs, _, out_ref = refs
    for i, r in enumerate(in_refs):
        out_ref[i] = r[...]


def weight_kernel(nx, sc_ref, v_ref, f_ref, out_ref):
    ny, tps, part, _ = out_ref.shape
    x = sc_ref[3]
    f = jnp.concatenate([f_ref[d] for d in range(nx)], axis=0)
    v = jnp.concatenate([v_ref[lax.rem(x + nx - d, nx)] for d in range(nx)], axis=0)
    term = lax.dot_general(v, f, TN, preferred_element_type=jnp.float32).T
    for t in range(tps):
        for y in range(ny):
            at = (t * ny + y) * part
            out_ref[y, t] = term[at : at + part].astype(out_ref.dtype)


def spread(piece, axes, count):
    copies = jnp.broadcast_to(piece[None], (count,) + piece.shape)
    return lax.all_to_all(copies, axes, split_axis=0, concat_axis=0, tiled=True)


def shift(a, axis, by):
    n = lax.axis_size(axis)
    return lax.ppermute(a, axis, [(i, (i + by) % n) for i in range(n)])


def per_device(queries, keys, values, out_grad, features, segment_ids):
    ny, nzh, nx, nzl, ncore = (lax.axis_size(a) for a in AXES)
    groups, tps = ny * nzh, nzl * ncore
    tokens = segment_ids.shape[0]
    rows = queries.shape[0]
    span = nx * rows
    g = lax.axis_index(("y", "zh"))
    x = lax.axis_index("x")
    bf16, f32 = jnp.bfloat16, jnp.float32

    own = jnp.concatenate([queries, out_grad], axis=1)
    qd = [own] + [shift(own, "x", d) for d in range(1, nx)]
    kv = spread(jnp.concatenate([keys, values], axis=1), ("y", "zh"), groups)
    kv = kv.reshape(groups * rows, 2 * HD)

    seg_q = lax.dynamic_slice_in_dim(segment_ids, g * span, span, 0)
    ids = jnp.arange(16, dtype=jnp.int32)
    firsts = jnp.sum((segment_ids[None, :] < ids[:, None]).astype(jnp.int32), axis=1)
    start = jnp.sum(jnp.where(seg_q[None, :] == ids[:, None], firsts[:, None], 0), axis=0)
    scalars = jnp.stack([g, start[0], start[span - 1], x]).astype(jnp.int32)
    start = start.reshape(1, span)

    smem = pl.BlockSpec(memory_space=pltpu.SMEM)
    vmem = pl.BlockSpec(memory_space=pltpu.VMEM)
    held = pl.BlockSpec(memory_space=pl.ANY)
    params = pltpu.CompilerParams(vmem_limit_bytes=VM * 1024 * 1024)

    wide = features.shape[1] // nx
    mine = pl.pallas_call(
        lambda *refs: regroup_kernel(nx, tps, *refs),
        out_shape=[jax.ShapeDtypeStruct((rows, wide), bf16)] * nx,
        in_specs=[smem, vmem],
        out_specs=[vmem] * nx,
        compiler_params=params,
    )(scalars, features)
    from_x = [mine[0]] + [shift(mine[d], "x", d) for d in range(1, nx)]

    stats = pl.pallas_call(
        lambda *refs: stats_kernel(nx, *refs),
        out_shape=jax.ShapeDtypeStruct((3, GROUP, span), f32),
        in_specs=[smem, vmem] + [vmem] * (nx + 1) + [held] * nx,
        out_specs=vmem,
        scratch_shapes=[pltpu.VMEM((3, GROUP, span), f32)],
        compiler_params=params,
    )(scalars, start, *qd, kv, *from_x)
    all_stats = spread(stats, "x", nx)
    dv_part = pl.pallas_call(
        lambda *refs: value_kernel(nx, *refs),
        out_shape=jax.ShapeDtypeStruct((groups * rows, HD), bf16),
        in_specs=[smem, vmem, vmem] + [vmem] * (nx + 1),
        out_specs=vmem,
        compiler_params=params,
    )(scalars, start, all_stats, *qd, kv)
    half = GROUP // 2
    dq_first = pl.pallas_call(
        lambda *refs: first_query_kernel(nx, range(half), *refs),
        out_shape=jax.ShapeDtypeStruct((nx, rows, half * HD), bf16),
        in_specs=[smem, vmem, vmem] + [vmem] * (nx + 1) + [held],
        out_specs=vmem,
        scratch_shapes=[pltpu.VMEM((half, HD, span), f32)],
        compiler_params=params,
    )(scalars, start, all_stats, *qd, kv, dv_part)

    f_all = pl.pallas_call(
        stack_kernel,
        out_shape=jax.ShapeDtypeStruct((nx, rows, wide), bf16),
        in_specs=[vmem] * nx + [held],
        out_specs=vmem,
        compiler_params=params,
    )(*from_x, dq_first)

    dv = lax.all_to_all(
        dv_part.reshape(groups, rows, HD), ("y", "zh"), split_axis=0, concat_axis=0, tiled=True
    )
    value_copies = pl.pallas_call(
        sum_kernel,
        out_shape=jax.ShapeDtypeStruct((nx, rows, HD), bf16),
        in_specs=[vmem, held],
        out_specs=vmem,
        compiler_params=params,
    )(dv, f_all)
    value_x = lax.all_to_all(value_copies, "x", split_axis=0, concat_axis=0, tiled=True)
    part = wide // (tps * ny)
    term = pl.pallas_call(
        lambda *refs: weight_kernel(nx, *refs),
        out_shape=jax.ShapeDtypeStruct((ny, tps, part, HD), bf16),
        in_specs=[smem, vmem, vmem],
        out_specs=vmem,
        compiler_params=params,
    )(scalars, value_x, f_all)
    pieces = lax.all_to_all(term, "y", split_axis=0, concat_axis=0, tiled=True)
    *dq_parts, done = pl.pallas_call(
        lambda *refs: last_query_kernel(nx, range(half, GROUP), *refs),
        out_shape=[jax.ShapeDtypeStruct((rows, GROUP * HD), bf16)] * nx
        + [jax.ShapeDtypeStruct((8, BLOCK), f32)],
        in_specs=[smem, vmem, vmem] + [vmem] * (nx + 2) + [held],
        out_specs=[vmem] * (nx + 1),
        scratch_shapes=[pltpu.VMEM((GROUP - half, HD, span), f32)],
        compiler_params=params,
    )(scalars, start, all_stats, *qd, kv, dq_first, term)
    row_copies = pl.pallas_call(
        sum_kernel,
        out_shape=jax.ShapeDtypeStruct((nzh, tps, part, HD), bf16),
        in_specs=[vmem, vmem],
        out_specs=vmem,
        compiler_params=params,
    )(pieces, done)
    turned = lax.all_to_all(
        row_copies.reshape(nzh * tps, part, HD),
        ("zh",) + TP, split_axis=0, concat_axis=0, tiled=True,
    ).reshape(nzh, tps, part, HD)
    own_rows = jnp.sum(turned.astype(f32), axis=0) * (1.0 / math.sqrt(tokens))
    own_rows = own_rows.astype(bf16).transpose(1, 0, 2).reshape(part, tps * HD)
    weight_grad = spread(own_rows, ("x", "y"), nx * ny)
    dq = dq_parts[0].astype(f32)
    for d in range(1, nx):
        dq = dq + shift(dq_parts[d], "x", -d).astype(f32)
    query_grads = dq.astype(bf16)
    return (query_grads, weight_grad.reshape(wide // tps * nx, tps * HD).astype(f32))


def solution(mesh):
    fine = Mesh(mesh.devices.reshape(DIMS), AXES)
    split = P(CTX, TP)
    return jax.shard_map(
        per_device,
        mesh=fine,
        in_specs=(split, split, split, split, P(CTX, None), P()),
        out_specs=(split, P(TP, None)),
        check_vma=False,
    )
```

```python
import math

import jax
import jax.numpy as jnp
from jax import lax
from jax.experimental import pallas as pl
from jax.experimental.pallas import tpu as pltpu
from jax.sharding import Mesh, PartitionSpec as P

HD = 128
GROUP = 4
DIMS = (8, 2, 4, 4, 2)
AXES = ("y", "zh", "x", "zl", "core")
CTX = ("y", "zh", "x")
TP = ("zl", "core")
BLOCK = 128
VM = 16
CHUNK = 256
PER = CHUNK // BLOCK
LOW = -1e30
FLOOR = -1e29
SCALE = HD ** (-0.5)
SCALE2 = SCALE * math.log2(math.e)
NT = (((1,), (1,)), ((), ()))
TN = (((0,), (0,)), ((), ()))


def lanes_of(ref_row, places):
    return jnp.concatenate([ref_row[:, pl.ds(p, BLOCK)] for p in places], axis=1)


def places_of(x, nx):
    return [pl.multiple_of(lax.rem(x + nx - d, nx) * BLOCK, BLOCK) for d in range(nx)]


def positions_of(g, x, nx):
    span = nx * BLOCK
    lane = lax.broadcasted_iota(jnp.int32, (1, BLOCK), 1)
    return jnp.concatenate([g * span + p + lane for p in places_of(x, nx)], axis=1)


def chunk_of(j, wide, kv_ref):
    at = pl.ds(pl.multiple_of(j * CHUNK, CHUNK), wide * CHUNK)
    return at, kv_ref[at, 0:HD], kv_ref[at, HD : 2 * HD]


def allowed_in(j, x, nx, pos_q, start):
    r = lax.broadcasted_iota(jnp.int32, (CHUNK, 1), 0)
    pos_k = (j * PER + r // BLOCK) * (nx * BLOCK) + x * BLOCK + r % BLOCK
    return (pos_k <= pos_q) & (pos_k >= start)


def head_of(q_refs, n):
    q = jnp.concatenate([r[:, n * HD : (n + 1) * HD] for r in q_refs], axis=0)
    do = jnp.concatenate([r[:, (GROUP + n) * HD : (GROUP + n + 1) * HD] for r in q_refs], axis=0)
    return q, do


def over_chunks(g, low, high, nx, step):
    width = PER * nx * BLOCK
    first, last = low // width, g // PER
    clear = jnp.minimum((high + width - 1) // width, last)
    pairs = (last - clear) // 2

    def masked(j, carry):
        step(j, 1, True)
        return carry

    def pair(i, carry):
        step(clear + 2 * i, 2, False)
        return carry

    def single(j, carry):
        step(j, 1, False)
        return carry

    lax.fori_loop(first, clear, masked, 0)
    lax.fori_loop(0, pairs, pair, 0)
    lax.fori_loop(clear + 2 * pairs, last, single, 0)
    step(last, 1, True)


def stats_kernel(nx, sc_ref, start_ref, *refs):
    q_refs, kv_ref, out_ref, st_ref = refs[:nx], refs[nx], refs[-2], refs[-1]
    g, low, high, x = sc_ref[0], sc_ref[1], sc_ref[2], sc_ref[3]
    span = nx * BLOCK
    pos_q = positions_of(g, x, nx)
    start = lanes_of(start_ref, places_of(x, nx))
    st_ref[0] = jnp.full((GROUP, span), FLOOR, jnp.float32)
    st_ref[1] = jnp.zeros((GROUP, span), jnp.float32)
    st_ref[2] = jnp.zeros((GROUP, span), jnp.float32)

    def step(j, wide, masked):
        _, k, v = chunk_of(j, wide, kv_ref)
        if masked:
            allowed = allowed_in(j, x, nx, pos_q, start)
        old = [[st_ref[k, n : n + 1, :] for k in range(3)] for n in range(GROUP)]
        new = []
        for n in range(GROUP):
            q, do = head_of(q_refs, n)
            s = lax.dot_general(k, q, NT, preferred_element_type=jnp.float32) * SCALE2
            if masked:
                s = jnp.where(allowed, s, LOW)
            dp = lax.dot_general(v, do, NT, preferred_element_type=jnp.float32)
            m_old, l_old, d_old = old[n]
            m = jnp.maximum(m_old, jnp.max(s, axis=0, keepdims=True))
            alpha = jnp.exp2(m_old - m)
            w = jnp.exp2(s - m)
            l = l_old * alpha + jnp.sum(w, axis=0, keepdims=True)
            new.append((m, l, d_old * alpha + jnp.sum(w * dp, axis=0, keepdims=True)))
        for n in range(GROUP):
            for k in range(3):
                st_ref[k, n : n + 1, :] = new[n][k]

    over_chunks(g, low, high, nx, step)
    for d, p in enumerate(places_of(x, nx)):
        for k in range(3):
            out_ref[k, :, pl.ds(p, BLOCK)] = st_ref[k, :, d * BLOCK : (d + 1) * BLOCK]


def combined(st_ref, places):
    nx = len(places)
    part = [[lanes_of(st_ref.at[i, k], places) for k in range(3)] for i in range(nx)]
    top = part[0][0]
    for i in range(1, nx):
        top = jnp.maximum(top, part[i][0])
    total = jnp.zeros_like(top)
    num = jnp.zeros_like(top)
    for i in range(nx):
        f = jnp.exp2(part[i][0] - top)
        total = total + part[i][1] * f
        num = num + part[i][2] * f
    return top + jnp.log2(total), num / total


def value_kernel(nx, sc_ref, start_ref, st_ref, *refs):
    q_refs, kv_ref, dv_ref = refs[:nx], refs[nx], refs[-1]
    g, low, high, x = sc_ref[0], sc_ref[1], sc_ref[2], sc_ref[3]
    places = places_of(x, nx)
    pos_q = positions_of(g, x, nx)
    start = lanes_of(start_ref, places)
    dv_ref[...] = jnp.zeros(dv_ref.shape, dv_ref.dtype)
    log_total, _ = combined(st_ref, places)

    def step(j, wide, masked):
        at, k, _ = chunk_of(j, wide, kv_ref)
        if masked:
            allowed = allowed_in(j, x, nx, pos_q, start)
        heads = [head_of(q_refs, n) for n in range(GROUP)]
        ps = []
        for n in range(GROUP):
            s = lax.dot_general(k, heads[n][0], NT, preferred_element_type=jnp.float32) * SCALE2
            if masked:
                s = jnp.where(allowed, s, LOW)
            ps.append(jnp.exp2(s - log_total[n : n + 1, :]).astype(jnp.bfloat16))
        dv = jnp.dot(
            jnp.concatenate(ps, axis=1),
            jnp.concatenate([do for _, do in heads], axis=0),
            preferred_element_type=jnp.float32,
        )
        dv_ref[at, :] = dv.astype(dv_ref.dtype)

    over_chunks(g, low, high, nx, step)


def query_kernel(nx, sc_ref, start_ref, st_ref, *refs):
    q_refs, kv_ref, (*dq_refs, done_ref, acc_ref) = refs[:nx], refs[nx], refs[nx + 2 :]
    done_ref[...] = jnp.zeros(done_ref.shape, done_ref.dtype)
    g, low, high, x = sc_ref[0], sc_ref[1], sc_ref[2], sc_ref[3]
    places = places_of(x, nx)
    pos_q = positions_of(g, x, nx)
    start = lanes_of(start_ref, places)
    acc_ref[...] = jnp.zeros(acc_ref.shape, jnp.float32)
    log_total, delta = combined(st_ref, places)

    def step(j, wide, masked):
        _, k, v = chunk_of(j, wide, kv_ref)
        if masked:
            allowed = allowed_in(j, x, nx, pos_q, start)
        for n in range(GROUP):
            q, do = head_of(q_refs, n)
            s = lax.dot_general(k, q, NT, preferred_element_type=jnp.float32) * SCALE2
            if masked:
                s = jnp.where(allowed, s, LOW)
            dp = lax.dot_general(v, do, NT, preferred_element_type=jnp.float32)
            p = jnp.exp2(s - log_total[n : n + 1, :])
            ds = (p * (dp - delta[n : n + 1, :])).astype(jnp.bfloat16)
            acc_ref[n] += lax.dot_general(k, ds, TN, preferred_element_type=jnp.float32)

    over_chunks(g, low, high, nx, step)
    for n in range(GROUP):
        dq = (acc_ref[n] * SCALE).T.astype(jnp.bfloat16)
        for d in range(nx):
            dq_refs[d][:, n * HD : (n + 1) * HD] = dq[d * BLOCK : (d + 1) * BLOCK]


def columns_for(to, nx, tps, f_ref):
    share = f_ref.shape[1] // tps
    wide = share // nx
    at = [pl.multiple_of(t * share + to * wide, wide) for t in range(tps)]
    return jnp.concatenate([f_ref[:, pl.ds(a, wide)] for a in at], axis=1)


def regroup_kernel(nx, tps, sc_ref, f_ref, *out_refs):
    for d, out_ref in enumerate(out_refs, 1):
        out_ref[...] = columns_for(lax.rem(sc_ref[3] + d, nx), nx, tps, f_ref)


def sum_kernel(in_ref, *refs):
    out_ref = refs[-1]
    total = in_ref[0].astype(jnp.float32)
    for i in range(1, in_ref.shape[0]):
        total = total + in_ref[i].astype(jnp.float32)
    total = total.astype(out_ref.dtype)
    for i in range(out_ref.shape[0]):
        out_ref[i] = total


def weight_kernel(nx, sc_ref, v_ref, own_ref, *refs):
    *f_refs, out_ref = refs
    ny, tps, part, _ = out_ref.shape
    x = sc_ref[3]
    f = jnp.concatenate([columns_for(x, nx, tps, own_ref)] + [r[...] for r in f_refs], axis=0)
    v = jnp.concatenate([v_ref[lax.rem(x + nx - d, nx)] for d in range(nx)], axis=0)
    term = lax.dot_general(v, f, TN, preferred_element_type=jnp.float32).T
    for t in range(tps):
        for y in range(ny):
            at = (t * ny + y) * part
            out_ref[y, t] = term[at : at + part].astype(out_ref.dtype)


def spread(piece, axes, count):
    copies = jnp.broadcast_to(piece[None], (count,) + piece.shape)
    return lax.all_to_all(copies, axes, split_axis=0, concat_axis=0, tiled=True)


def shift(a, axis, by):
    n = lax.axis_size(axis)
    return lax.ppermute(a, axis, [(i, (i + by) % n) for i in range(n)])


def per_device(queries, keys, values, out_grad, features, segment_ids):
    ny, nzh, nx, nzl, ncore = (lax.axis_size(a) for a in AXES)
    groups, tps = ny * nzh, nzl * ncore
    tokens = segment_ids.shape[0]
    rows = queries.shape[0]
    span = nx * rows
    g = lax.axis_index(("y", "zh"))
    x = lax.axis_index("x")
    bf16, f32 = jnp.bfloat16, jnp.float32

    own = jnp.concatenate([queries, out_grad], axis=1)
    qd = [own] + [shift(own, "x", d) for d in range(1, nx)]
    kv = spread(jnp.concatenate([keys, values], axis=1), ("y", "zh"), groups)
    kv = kv.reshape(groups * rows, 2 * HD)

    seg_q = lax.dynamic_slice_in_dim(segment_ids, g * span, span, 0)
    ids = jnp.arange(16, dtype=jnp.int32)
    firsts = jnp.sum((segment_ids[None, :] < ids[:, None]).astype(jnp.int32), axis=1)
    start = jnp.sum(jnp.where(seg_q[None, :] == ids[:, None], firsts[:, None], 0), axis=0)
    scalars = jnp.stack([g, start[0], start[span - 1], x]).astype(jnp.int32)
    start = start.reshape(1, span)

    smem = pl.BlockSpec(memory_space=pltpu.SMEM)
    vmem = pl.BlockSpec(memory_space=pltpu.VMEM)
    unread = pl.BlockSpec(memory_space=pl.ANY)
    params = pltpu.CompilerParams(vmem_limit_bytes=VM * 1024 * 1024)

    wide = features.shape[1] // nx
    mine = pl.pallas_call(
        lambda *refs: regroup_kernel(nx, tps, *refs),
        out_shape=[jax.ShapeDtypeStruct((rows, wide), bf16)] * (nx - 1),
        in_specs=[smem, vmem],
        out_specs=[vmem] * (nx - 1),
        compiler_params=params,
    )(scalars, features)
    from_x = [shift(mine[d - 1], "x", d) for d in range(1, nx)]

    stats = pl.pallas_call(
        lambda *refs: stats_kernel(nx, *refs),
        out_shape=jax.ShapeDtypeStruct((3, GROUP, span), f32),
        in_specs=[smem, vmem] + [vmem] * (nx + 1),
        out_specs=vmem,
        scratch_shapes=[pltpu.VMEM((3, GROUP, span), f32)],
        compiler_params=params,
    )(scalars, start, *qd, kv)
    all_stats = spread(stats, "x", nx)
    dv_part = pl.pallas_call(
        lambda *refs: value_kernel(nx, *refs),
        out_shape=jax.ShapeDtypeStruct((groups * rows, HD), bf16),
        in_specs=[smem, vmem, vmem] + [vmem] * (nx + 1) + [unread] * (nx - 1),
        out_specs=vmem,
        compiler_params=params,
    )(scalars, start, all_stats, *qd, kv, *from_x)
    *dq_parts, done = pl.pallas_call(
        lambda *refs: query_kernel(nx, *refs),
        out_shape=[jax.ShapeDtypeStruct((rows, GROUP * HD), bf16)] * nx
        + [jax.ShapeDtypeStruct((8, BLOCK), f32)],
        in_specs=[smem, vmem, vmem] + [vmem] * (nx + 1) + [unread],
        out_specs=[vmem] * (nx + 1),
        scratch_shapes=[pltpu.VMEM((GROUP, HD, span), f32)],
        compiler_params=params,
    )(scalars, start, all_stats, *qd, kv, dv_part)

    dv = lax.all_to_all(
        dv_part.reshape(groups, rows, HD), ("y", "zh"), split_axis=0, concat_axis=0, tiled=True
    )
    value_copies = pl.pallas_call(
        sum_kernel,
        out_shape=jax.ShapeDtypeStruct((nx, rows, HD), bf16),
        in_specs=[vmem, vmem],
        out_specs=vmem,
        compiler_params=params,
    )(dv, done)
    value_x = lax.all_to_all(value_copies, "x", split_axis=0, concat_axis=0, tiled=True)
    part = wide // (tps * ny)
    term = pl.pallas_call(
        lambda *refs: weight_kernel(nx, *refs),
        out_shape=jax.ShapeDtypeStruct((ny, tps, part, HD), bf16),
        in_specs=[smem] + [vmem] * (nx + 1),
        out_specs=vmem,
        compiler_params=params,
    )(scalars, value_x, features, *from_x)
    pieces = lax.all_to_all(term, "y", split_axis=0, concat_axis=0, tiled=True)
    summed = jnp.sum(pieces.astype(f32), axis=0).astype(bf16)
    turned = lax.all_to_all(
        jnp.broadcast_to(summed[None], (nzh,) + summed.shape).reshape(nzh * tps, part, HD),
        ("zh",) + TP, split_axis=0, concat_axis=0, tiled=True,
    ).reshape(nzh, tps, part, HD)
    own_rows = jnp.sum(turned.astype(f32), axis=0) * (1.0 / math.sqrt(tokens))
    own_rows = own_rows.astype(bf16).transpose(1, 0, 2).reshape(part, tps * HD)
    weight_grad = spread(own_rows, ("x", "y"), nx * ny)
    dq = dq_parts[0].astype(f32)
    for d in range(1, nx):
        dq = dq + shift(dq_parts[d], "x", -d).astype(f32)
    query_grads = dq.astype(bf16)
    return (query_grads, weight_grad.reshape(wide // tps * nx, tps * HD).astype(f32))


def solution(mesh):
    fine = Mesh(mesh.devices.reshape(DIMS), AXES)
    split = P(CTX, TP)
    return jax.shard_map(
        per_device,
        mesh=fine,
        in_specs=(split, split, split, split, P(CTX, None), P()),
        out_specs=(split, P(TP, None)),
        check_vma=False,
    )
```

```python
import math

import jax
import jax.numpy as jnp
from jax import lax
from jax.experimental import pallas as pl
from jax.experimental.pallas import tpu as pltpu
from jax.sharding import Mesh, PartitionSpec as P

HD = 128
GROUP = 4
DIMS = (8, 2, 4, 4, 2)
AXES = ("y", "zh", "x", "zl", "core")
CTX = ("y", "zh", "x")
TP = ("zl", "core")
BLOCK = 128
VM = 16
CHUNK = 256
PER = CHUNK // BLOCK
LOW = -1e30
FLOOR = -1e29
SCALE = HD ** (-0.5)
SCALE2 = SCALE * math.log2(math.e)
NT = (((1,), (1,)), ((), ()))
TN = (((0,), (0,)), ((), ()))


def lanes_of(ref_row, places):
    return jnp.concatenate([ref_row[:, pl.ds(p, BLOCK)] for p in places], axis=1)


def places_of(x, nx):
    return [pl.multiple_of(lax.rem(x + nx - d, nx) * BLOCK, BLOCK) for d in range(nx)]


def positions_of(g, x, nx):
    span = nx * BLOCK
    lane = lax.broadcasted_iota(jnp.int32, (1, BLOCK), 1)
    return jnp.concatenate([g * span + p + lane for p in places_of(x, nx)], axis=1)


def chunk_of(j, wide, kv_ref):
    at = pl.ds(pl.multiple_of(j * CHUNK, CHUNK), wide * CHUNK)
    return at, kv_ref[at, 0:HD], kv_ref[at, HD : 2 * HD]


def allowed_in(j, x, nx, pos_q, start):
    r = lax.broadcasted_iota(jnp.int32, (CHUNK, 1), 0)
    pos_k = (j * PER + r // BLOCK) * (nx * BLOCK) + x * BLOCK + r % BLOCK
    return (pos_k <= pos_q) & (pos_k >= start)


def head_of(q_refs, n):
    q = jnp.concatenate([r[:, n * HD : (n + 1) * HD] for r in q_refs], axis=0)
    do = jnp.concatenate([r[:, (GROUP + n) * HD : (GROUP + n + 1) * HD] for r in q_refs], axis=0)
    return q, do


def over_chunks(g, low, high, nx, step):
    width = PER * nx * BLOCK
    first, last = low // width, g // PER
    clear = jnp.minimum((high + width - 1) // width, last)
    pairs = (last - clear) // 2

    def masked(j, carry):
        step(j, 1, True)
        return carry

    def pair(i, carry):
        step(clear + 2 * i, 2, False)
        return carry

    def single(j, carry):
        step(j, 1, False)
        return carry

    lax.fori_loop(first, clear, masked, 0)
    lax.fori_loop(0, pairs, pair, 0)
    lax.fori_loop(clear + 2 * pairs, last, single, 0)
    step(last, 1, True)


def stats_kernel(nx, sc_ref, start_ref, *refs):
    q_refs, kv_ref, out_ref, st_ref = refs[:nx], refs[nx], refs[-2], refs[-1]
    g, low, high, x = sc_ref[0], sc_ref[1], sc_ref[2], sc_ref[3]
    span = nx * BLOCK
    pos_q = positions_of(g, x, nx)
    start = lanes_of(start_ref, places_of(x, nx))
    st_ref[0] = jnp.full((GROUP, span), FLOOR, jnp.float32)
    st_ref[1] = jnp.zeros((GROUP, span), jnp.float32)
    st_ref[2] = jnp.zeros((GROUP, span), jnp.float32)

    def step(j, wide, masked):
        _, k, v = chunk_of(j, wide, kv_ref)
        if masked:
            allowed = allowed_in(j, x, nx, pos_q, start)
        old = [[st_ref[k, n : n + 1, :] for k in range(3)] for n in range(GROUP)]
        new = []
        for n in range(GROUP):
            q, do = head_of(q_refs, n)
            s = lax.dot_general(k, q, NT, preferred_element_type=jnp.float32) * SCALE2
            if masked:
                s = jnp.where(allowed, s, LOW)
            dp = lax.dot_general(v, do, NT, preferred_element_type=jnp.float32)
            m_old, l_old, d_old = old[n]
            m = jnp.maximum(m_old, jnp.max(s, axis=0, keepdims=True))
            alpha = jnp.exp2(m_old - m)
            w = jnp.exp2(s - m)
            l = l_old * alpha + jnp.sum(w, axis=0, keepdims=True)
            new.append((m, l, d_old * alpha + jnp.sum(w * dp, axis=0, keepdims=True)))
        for n in range(GROUP):
            for k in range(3):
                st_ref[k, n : n + 1, :] = new[n][k]

    over_chunks(g, low, high, nx, step)
    for d, p in enumerate(places_of(x, nx)):
        for k in range(3):
            out_ref[k, :, pl.ds(p, BLOCK)] = st_ref[k, :, d * BLOCK : (d + 1) * BLOCK]


def combined(st_ref, places):
    nx = len(places)
    part = [[lanes_of(st_ref.at[i, k], places) for k in range(3)] for i in range(nx)]
    top = part[0][0]
    for i in range(1, nx):
        top = jnp.maximum(top, part[i][0])
    total = jnp.zeros_like(top)
    num = jnp.zeros_like(top)
    for i in range(nx):
        f = jnp.exp2(part[i][0] - top)
        total = total + part[i][1] * f
        num = num + part[i][2] * f
    return top + jnp.log2(total), num / total


def value_kernel(nx, sc_ref, start_ref, st_ref, *refs):
    q_refs, kv_ref, dv_ref = refs[:nx], refs[nx], refs[nx + 1]
    g, low, high, x = sc_ref[0], sc_ref[1], sc_ref[2], sc_ref[3]
    places = places_of(x, nx)
    pos_q = positions_of(g, x, nx)
    start = lanes_of(start_ref, places)
    dv_ref[...] = jnp.zeros(dv_ref.shape, dv_ref.dtype)
    log_total, _ = combined(st_ref, places)

    def step(j, wide, masked):
        at, k, _ = chunk_of(j, wide, kv_ref)
        if masked:
            allowed = allowed_in(j, x, nx, pos_q, start)
        heads = [head_of(q_refs, n) for n in range(GROUP)]
        ps = []
        for n in range(GROUP):
            s = lax.dot_general(k, heads[n][0], NT, preferred_element_type=jnp.float32) * SCALE2
            if masked:
                s = jnp.where(allowed, s, LOW)
            ps.append(jnp.exp2(s - log_total[n : n + 1, :]).astype(jnp.bfloat16))
        dv = jnp.dot(
            jnp.concatenate(ps, axis=1),
            jnp.concatenate([do for _, do in heads], axis=0),
            preferred_element_type=jnp.float32,
        )
        dv_ref[at, :] = dv.astype(dv_ref.dtype)

    over_chunks(g, low, high, nx, step)


def query_kernel(nx, sc_ref, start_ref, st_ref, *refs):
    q_refs, kv_ref, (dq_ref, done_ref, acc_ref) = refs[:nx], refs[nx], refs[nx + 2 :]
    done_ref[...] = jnp.zeros(done_ref.shape, done_ref.dtype)
    g, low, high, x = sc_ref[0], sc_ref[1], sc_ref[2], sc_ref[3]
    places = places_of(x, nx)
    pos_q = positions_of(g, x, nx)
    start = lanes_of(start_ref, places)
    acc_ref[...] = jnp.zeros(acc_ref.shape, jnp.float32)
    log_total, delta = combined(st_ref, places)

    def step(j, wide, masked):
        _, k, v = chunk_of(j, wide, kv_ref)
        if masked:
            allowed = allowed_in(j, x, nx, pos_q, start)
        for n in range(GROUP):
            q, do = head_of(q_refs, n)
            s = lax.dot_general(k, q, NT, preferred_element_type=jnp.float32) * SCALE2
            if masked:
                s = jnp.where(allowed, s, LOW)
            dp = lax.dot_general(v, do, NT, preferred_element_type=jnp.float32)
            p = jnp.exp2(s - log_total[n : n + 1, :])
            ds = (p * (dp - delta[n : n + 1, :])).astype(jnp.bfloat16)
            acc_ref[n] += lax.dot_general(k, ds, TN, preferred_element_type=jnp.float32)

    over_chunks(g, low, high, nx, step)
    for n in range(GROUP):
        dq = (acc_ref[n] * SCALE).T.astype(jnp.bfloat16)
        for d in range(nx):
            dq_ref[d, :, n * HD : (n + 1) * HD] = dq[d * BLOCK : (d + 1) * BLOCK]


def regroup_kernel(nx, tps, sc_ref, f_ref, *out_refs):
    x = sc_ref[3]
    share = f_ref.shape[1] // tps
    wide = share // nx
    for d, out_ref in enumerate(out_refs):
        to = lax.rem(x + d, nx) * wide
        for t in range(tps):
            at = pl.multiple_of(t * share + to, wide)
            out_ref[:, t * wide : (t + 1) * wide] = f_ref[:, pl.ds(at, wide)]


def sum_kernel(in_ref, *refs):
    out_ref = refs[-1]
    total = in_ref[0].astype(jnp.float32)
    for i in range(1, in_ref.shape[0]):
        total = total + in_ref[i].astype(jnp.float32)
    total = total.astype(out_ref.dtype)
    for i in range(out_ref.shape[0]):
        out_ref[i] = total


def weight_kernel(nx, sc_ref, v_ref, *refs):
    f_refs, out_ref = refs[:nx], refs[nx]
    ny, tps, part, _ = out_ref.shape
    x = sc_ref[3]
    f = jnp.concatenate([r[...] for r in f_refs], axis=0)
    v = jnp.concatenate([v_ref[lax.rem(x + nx - d, nx)] for d in range(nx)], axis=0)
    term = lax.dot_general(v, f, TN, preferred_element_type=jnp.float32).T
    for t in range(tps):
        for y in range(ny):
            at = (t * ny + y) * part
            out_ref[y, t] = term[at : at + part].astype(out_ref.dtype)


def spread(piece, axes, count):
    copies = jnp.broadcast_to(piece[None], (count,) + piece.shape)
    return lax.all_to_all(copies, axes, split_axis=0, concat_axis=0, tiled=True)


def shift(a, axis, by):
    n = lax.axis_size(axis)
    return lax.ppermute(a, axis, [(i, (i + by) % n) for i in range(n)])


def per_device(queries, keys, values, out_grad, features, segment_ids):
    ny, nzh, nx, nzl, ncore = (lax.axis_size(a) for a in AXES)
    groups, tps = ny * nzh, nzl * ncore
    tokens = segment_ids.shape[0]
    rows = queries.shape[0]
    span = nx * rows
    g = lax.axis_index(("y", "zh"))
    x = lax.axis_index("x")
    bf16, f32 = jnp.bfloat16, jnp.float32

    own = jnp.concatenate([queries, out_grad], axis=1)
    qd = [own] + [shift(own, "x", d) for d in range(1, nx)]
    kv = spread(jnp.concatenate([keys, values], axis=1), ("y", "zh"), groups)
    kv = kv.reshape(groups * rows, 2 * HD)

    seg_q = lax.dynamic_slice_in_dim(segment_ids, g * span, span, 0)
    ids = jnp.arange(16, dtype=jnp.int32)
    firsts = jnp.sum((segment_ids[None, :] < ids[:, None]).astype(jnp.int32), axis=1)
    start = jnp.sum(jnp.where(seg_q[None, :] == ids[:, None], firsts[:, None], 0), axis=0)
    scalars = jnp.stack([g, start[0], start[span - 1], x]).astype(jnp.int32)
    start = start.reshape(1, span)

    smem = pl.BlockSpec(memory_space=pltpu.SMEM)
    vmem = pl.BlockSpec(memory_space=pltpu.VMEM)
    unread = pl.BlockSpec(memory_space=pl.ANY)
    params = pltpu.CompilerParams(vmem_limit_bytes=VM * 1024 * 1024)

    wide = features.shape[1] // nx
    mine = pl.pallas_call(
        lambda *refs: regroup_kernel(nx, tps, *refs),
        out_shape=[jax.ShapeDtypeStruct((rows, wide), bf16)] * nx,
        in_specs=[smem, vmem],
        out_specs=[vmem] * nx,
        compiler_params=params,
    )(scalars, features)
    from_x = [mine[0]] + [shift(mine[d], "x", d) for d in range(1, nx)]

    stats = pl.pallas_call(
        lambda *refs: stats_kernel(nx, *refs),
        out_shape=jax.ShapeDtypeStruct((3, GROUP, span), f32),
        in_specs=[smem, vmem] + [vmem] * (nx + 1) + [unread] * nx,
        out_specs=vmem,
        scratch_shapes=[pltpu.VMEM((3, GROUP, span), f32)],
        compiler_params=params,
    )(scalars, start, *qd, kv, *from_x)
    all_stats = spread(stats, "x", nx)
    dv_part = pl.pallas_call(
        lambda *refs: value_kernel(nx, *refs),
        out_shape=jax.ShapeDtypeStruct((groups * rows, HD), bf16),
        in_specs=[smem, vmem, vmem] + [vmem] * (nx + 1),
        out_specs=vmem,
        compiler_params=params,
    )(scalars, start, all_stats, *qd, kv)
    dq_parts, done = pl.pallas_call(
        lambda *refs: query_kernel(nx, *refs),
        out_shape=(
            jax.ShapeDtypeStruct((nx, rows, GROUP * HD), bf16),
            jax.ShapeDtypeStruct((8, BLOCK), f32),
        ),
        in_specs=[smem, vmem, vmem] + [vmem] * (nx + 1) + [unread],
        out_specs=(vmem, vmem),
        scratch_shapes=[pltpu.VMEM((GROUP, HD, span), f32)],
        compiler_params=params,
    )(scalars, start, all_stats, *qd, kv, dv_part)

    dv = lax.all_to_all(
        dv_part.reshape(groups, rows, HD), ("y", "zh"), split_axis=0, concat_axis=0, tiled=True
    )
    value_copies = pl.pallas_call(
        sum_kernel,
        out_shape=jax.ShapeDtypeStruct((nx, rows, HD), bf16),
        in_specs=[vmem, vmem],
        out_specs=vmem,
        compiler_params=params,
    )(dv, done)
    value_x = lax.all_to_all(value_copies, "x", split_axis=0, concat_axis=0, tiled=True)
    part = wide // (tps * ny)
    term = pl.pallas_call(
        lambda *refs: weight_kernel(nx, *refs),
        out_shape=jax.ShapeDtypeStruct((ny, tps, part, HD), bf16),
        in_specs=[smem] + [vmem] * (nx + 1),
        out_specs=vmem,
        compiler_params=params,
    )(scalars, value_x, *from_x)
    pieces = lax.all_to_all(term, "y", split_axis=0, concat_axis=0, tiled=True)
    summed = jnp.sum(pieces.astype(f32), axis=0).astype(bf16)
    turned = lax.all_to_all(
        jnp.broadcast_to(summed[None], (nzh,) + summed.shape).reshape(nzh * tps, part, HD),
        ("zh",) + TP, split_axis=0, concat_axis=0, tiled=True,
    ).reshape(nzh, tps, part, HD)
    own_rows = jnp.sum(turned.astype(f32), axis=0) * (1.0 / math.sqrt(tokens))
    own_rows = own_rows.astype(bf16).transpose(1, 0, 2).reshape(part, tps * HD)
    weight_grad = spread(own_rows, ("x", "y"), nx * ny)
    dq = dq_parts[0].astype(f32)
    for d in range(1, nx):
        dq = dq + shift(dq_parts[d], "x", -d).astype(f32)
    query_grads = dq.astype(bf16)
    return (query_grads, weight_grad.reshape(wide // tps * nx, tps * HD).astype(f32))


def solution(mesh):
    fine = Mesh(mesh.devices.reshape(DIMS), AXES)
    split = P(CTX, TP)
    return jax.shard_map(
        per_device,
        mesh=fine,
        in_specs=(split, split, split, split, P(CTX, None), P()),
        out_specs=(split, P(TP, None)),
        check_vma=False,
    )
```

```python
import math

import jax
import jax.numpy as jnp
from jax import lax
from jax.experimental import pallas as pl
from jax.experimental.pallas import tpu as pltpu
from jax.sharding import Mesh, PartitionSpec as P

HD = 128
GROUP = 4
DIMS = (8, 2, 4, 4, 2)
AXES = ("y", "zh", "x", "zl", "core")
CTX = ("y", "zh", "x")
TP = ("zl", "core")
BLOCK = 128
VM = 16
CHUNK = 256
PER = CHUNK // BLOCK
LOW = -1e30
FLOOR = -1e29
SCALE = HD ** (-0.5)
SCALE2 = SCALE * math.log2(math.e)
NT = (((1,), (1,)), ((), ()))
TN = (((0,), (0,)), ((), ()))


def lanes_of(ref_row, places):
    return jnp.concatenate([ref_row[:, pl.ds(p, BLOCK)] for p in places], axis=1)


def places_of(x, nx):
    return [pl.multiple_of(lax.rem(x + nx - d, nx) * BLOCK, BLOCK) for d in range(nx)]


def positions_of(g, x, nx):
    span = nx * BLOCK
    lane = lax.broadcasted_iota(jnp.int32, (1, BLOCK), 1)
    return jnp.concatenate([g * span + p + lane for p in places_of(x, nx)], axis=1)


def chunk_of(j, wide, kv_ref):
    at = pl.ds(pl.multiple_of(j * CHUNK, CHUNK), wide * CHUNK)
    return at, kv_ref[at, 0:HD], kv_ref[at, HD : 2 * HD]


def allowed_in(j, x, nx, pos_q, start):
    r = lax.broadcasted_iota(jnp.int32, (CHUNK, 1), 0)
    pos_k = (j * PER + r // BLOCK) * (nx * BLOCK) + x * BLOCK + r % BLOCK
    return (pos_k <= pos_q) & (pos_k >= start)


def head_of(q_refs, n):
    q = jnp.concatenate([r[:, n * HD : (n + 1) * HD] for r in q_refs], axis=0)
    do = jnp.concatenate([r[:, (GROUP + n) * HD : (GROUP + n + 1) * HD] for r in q_refs], axis=0)
    return q, do


def over_chunks(g, low, high, nx, step):
    width = PER * nx * BLOCK
    first, last = low // width, g // PER
    clear = jnp.minimum((high + width - 1) // width, last)
    pairs = (last - clear) // 2

    def masked(j, carry):
        step(j, 1, True)
        return carry

    def pair(i, carry):
        step(clear + 2 * i, 2, False)
        return carry

    def single(j, carry):
        step(j, 1, False)
        return carry

    lax.fori_loop(first, clear, masked, 0)
    lax.fori_loop(0, pairs, pair, 0)
    lax.fori_loop(clear + 2 * pairs, last, single, 0)
    step(last, 1, True)


def stats_kernel(nx, sc_ref, start_ref, *refs):
    q_refs, kv_ref, out_ref, st_ref = refs[:nx], refs[nx], refs[-2], refs[-1]
    g, low, high, x = sc_ref[0], sc_ref[1], sc_ref[2], sc_ref[3]
    span = nx * BLOCK
    pos_q = positions_of(g, x, nx)
    start = lanes_of(start_ref, places_of(x, nx))
    st_ref[0] = jnp.full((GROUP, span), FLOOR, jnp.float32)
    st_ref[1] = jnp.zeros((GROUP, span), jnp.float32)
    st_ref[2] = jnp.zeros((GROUP, span), jnp.float32)

    def step(j, wide, masked):
        _, k, v = chunk_of(j, wide, kv_ref)
        if masked:
            allowed = allowed_in(j, x, nx, pos_q, start)
        old = [[st_ref[k, n : n + 1, :] for k in range(3)] for n in range(GROUP)]
        new = []
        for n in range(GROUP):
            q, do = head_of(q_refs, n)
            s = lax.dot_general(k, q, NT, preferred_element_type=jnp.float32) * SCALE2
            if masked:
                s = jnp.where(allowed, s, LOW)
            dp = lax.dot_general(v, do, NT, preferred_element_type=jnp.float32)
            m_old, l_old, d_old = old[n]
            m = jnp.maximum(m_old, jnp.max(s, axis=0, keepdims=True))
            alpha = jnp.exp2(m_old - m)
            w = jnp.exp2(s - m)
            l = l_old * alpha + jnp.sum(w, axis=0, keepdims=True)
            new.append((m, l, d_old * alpha + jnp.sum(w * dp, axis=0, keepdims=True)))
        for n in range(GROUP):
            for k in range(3):
                st_ref[k, n : n + 1, :] = new[n][k]

    over_chunks(g, low, high, nx, step)
    for d, p in enumerate(places_of(x, nx)):
        for k in range(3):
            out_ref[k, :, pl.ds(p, BLOCK)] = st_ref[k, :, d * BLOCK : (d + 1) * BLOCK]


def combined(st_ref, places):
    nx = len(places)
    part = [[lanes_of(st_ref.at[i, k], places) for k in range(3)] for i in range(nx)]
    top = part[0][0]
    for i in range(1, nx):
        top = jnp.maximum(top, part[i][0])
    total = jnp.zeros_like(top)
    num = jnp.zeros_like(top)
    for i in range(nx):
        f = jnp.exp2(part[i][0] - top)
        total = total + part[i][1] * f
        num = num + part[i][2] * f
    return top + jnp.log2(total), num / total


def value_kernel(nx, sc_ref, start_ref, st_ref, *refs):
    q_refs, kv_ref, dv_ref = refs[:nx], refs[nx], refs[-1]
    g, low, high, x = sc_ref[0], sc_ref[1], sc_ref[2], sc_ref[3]
    places = places_of(x, nx)
    pos_q = positions_of(g, x, nx)
    start = lanes_of(start_ref, places)
    dv_ref[...] = jnp.zeros(dv_ref.shape, dv_ref.dtype)
    log_total, _ = combined(st_ref, places)

    def step(j, wide, masked):
        at, k, _ = chunk_of(j, wide, kv_ref)
        if masked:
            allowed = allowed_in(j, x, nx, pos_q, start)
        heads = [head_of(q_refs, n) for n in range(GROUP)]
        ps = []
        for n in range(GROUP):
            s = lax.dot_general(k, heads[n][0], NT, preferred_element_type=jnp.float32) * SCALE2
            if masked:
                s = jnp.where(allowed, s, LOW)
            ps.append(jnp.exp2(s - log_total[n : n + 1, :]).astype(jnp.bfloat16))
        dv = jnp.dot(
            jnp.concatenate(ps, axis=1),
            jnp.concatenate([do for _, do in heads], axis=0),
            preferred_element_type=jnp.float32,
        )
        dv_ref[at, :] = dv.astype(dv_ref.dtype)

    over_chunks(g, low, high, nx, step)


def query_kernel(nx, sc_ref, start_ref, st_ref, *refs):
    q_refs, kv_ref, (dq_ref, done_ref, acc_ref) = refs[:nx], refs[nx], refs[nx + 2 :]
    done_ref[...] = jnp.zeros(done_ref.shape, done_ref.dtype)
    g, low, high, x = sc_ref[0], sc_ref[1], sc_ref[2], sc_ref[3]
    places = places_of(x, nx)
    pos_q = positions_of(g, x, nx)
    start = lanes_of(start_ref, places)
    acc_ref[...] = jnp.zeros(acc_ref.shape, jnp.float32)
    log_total, delta = combined(st_ref, places)

    def step(j, wide, masked):
        _, k, v = chunk_of(j, wide, kv_ref)
        if masked:
            allowed = allowed_in(j, x, nx, pos_q, start)
        for n in range(GROUP):
            q, do = head_of(q_refs, n)
            s = lax.dot_general(k, q, NT, preferred_element_type=jnp.float32) * SCALE2
            if masked:
                s = jnp.where(allowed, s, LOW)
            dp = lax.dot_general(v, do, NT, preferred_element_type=jnp.float32)
            p = jnp.exp2(s - log_total[n : n + 1, :])
            ds = (p * (dp - delta[n : n + 1, :])).astype(jnp.bfloat16)
            acc_ref[n] += lax.dot_general(k, ds, TN, preferred_element_type=jnp.float32)

    over_chunks(g, low, high, nx, step)
    for n in range(GROUP):
        dq = (acc_ref[n] * SCALE).T.astype(jnp.bfloat16)
        for d in range(nx):
            dq_ref[d, :, n * HD : (n + 1) * HD] = dq[d * BLOCK : (d + 1) * BLOCK]


def regroup_kernel(nx, tps, sc_ref, f_ref, *out_refs):
    x = sc_ref[3]
    share = f_ref.shape[1] // tps
    wide = share // nx
    for d, out_ref in enumerate(out_refs):
        to = lax.rem(x + d, nx) * wide
        for t in range(tps):
            at = pl.multiple_of(t * share + to, wide)
            out_ref[:, t * wide : (t + 1) * wide] = f_ref[:, pl.ds(at, wide)]


def sum_kernel(in_ref, *refs):
    out_ref = refs[-1]
    total = in_ref[0].astype(jnp.float32)
    for i in range(1, in_ref.shape[0]):
        total = total + in_ref[i].astype(jnp.float32)
    total = total.astype(out_ref.dtype)
    for i in range(out_ref.shape[0]):
        out_ref[i] = total


def weight_kernel(nx, sc_ref, v_ref, *refs):
    f_refs, out_ref = refs[:nx], refs[nx]
    ny, tps, part, _ = out_ref.shape
    x = sc_ref[3]
    f = jnp.concatenate([r[...] for r in f_refs], axis=0)
    v = jnp.concatenate([v_ref[lax.rem(x + nx - d, nx)] for d in range(nx)], axis=0)
    term = lax.dot_general(v, f, TN, preferred_element_type=jnp.float32).T
    for t in range(tps):
        for y in range(ny):
            at = (t * ny + y) * part
            out_ref[y, t] = term[at : at + part].astype(out_ref.dtype)


def spread(piece, axes, count):
    copies = jnp.broadcast_to(piece[None], (count,) + piece.shape)
    return lax.all_to_all(copies, axes, split_axis=0, concat_axis=0, tiled=True)


def shift(a, axis, by):
    n = lax.axis_size(axis)
    return lax.ppermute(a, axis, [(i, (i + by) % n) for i in range(n)])


def per_device(queries, keys, values, out_grad, features, segment_ids):
    ny, nzh, nx, nzl, ncore = (lax.axis_size(a) for a in AXES)
    groups, tps = ny * nzh, nzl * ncore
    tokens = segment_ids.shape[0]
    rows = queries.shape[0]
    span = nx * rows
    g = lax.axis_index(("y", "zh"))
    x = lax.axis_index("x")
    bf16, f32 = jnp.bfloat16, jnp.float32

    own = jnp.concatenate([queries, out_grad], axis=1)
    qd = [own] + [shift(own, "x", d) for d in range(1, nx)]
    kv = spread(jnp.concatenate([keys, values], axis=1), ("y", "zh"), groups)
    kv = kv.reshape(groups * rows, 2 * HD)

    seg_q = lax.dynamic_slice_in_dim(segment_ids, g * span, span, 0)
    ids = jnp.arange(16, dtype=jnp.int32)
    firsts = jnp.sum((segment_ids[None, :] < ids[:, None]).astype(jnp.int32), axis=1)
    start = jnp.sum(jnp.where(seg_q[None, :] == ids[:, None], firsts[:, None], 0), axis=0)
    scalars = jnp.stack([g, start[0], start[span - 1], x]).astype(jnp.int32)
    start = start.reshape(1, span)

    smem = pl.BlockSpec(memory_space=pltpu.SMEM)
    vmem = pl.BlockSpec(memory_space=pltpu.VMEM)
    unread = pl.BlockSpec(memory_space=pl.ANY)
    params = pltpu.CompilerParams(vmem_limit_bytes=VM * 1024 * 1024)

    wide = features.shape[1] // nx
    mine = pl.pallas_call(
        lambda *refs: regroup_kernel(nx, tps, *refs),
        out_shape=[jax.ShapeDtypeStruct((rows, wide), bf16)] * nx,
        in_specs=[smem, vmem],
        out_specs=[vmem] * nx,
        compiler_params=params,
    )(scalars, features)
    from_x = [mine[0]] + [shift(mine[d], "x", d) for d in range(1, nx)]

    stats = pl.pallas_call(
        lambda *refs: stats_kernel(nx, *refs),
        out_shape=jax.ShapeDtypeStruct((3, GROUP, span), f32),
        in_specs=[smem, vmem] + [vmem] * (nx + 1),
        out_specs=vmem,
        scratch_shapes=[pltpu.VMEM((3, GROUP, span), f32)],
        compiler_params=params,
    )(scalars, start, *qd, kv)
    all_stats = spread(stats, "x", nx)
    dv_part = pl.pallas_call(
        lambda *refs: value_kernel(nx, *refs),
        out_shape=jax.ShapeDtypeStruct((groups * rows, HD), bf16),
        in_specs=[smem, vmem, vmem] + [vmem] * (nx + 1) + [unread] * nx,
        out_specs=vmem,
        compiler_params=params,
    )(scalars, start, all_stats, *qd, kv, *from_x)
    dq_parts, done = pl.pallas_call(
        lambda *refs: query_kernel(nx, *refs),
        out_shape=(
            jax.ShapeDtypeStruct((nx, rows, GROUP * HD), bf16),
            jax.ShapeDtypeStruct((8, BLOCK), f32),
        ),
        in_specs=[smem, vmem, vmem] + [vmem] * (nx + 1) + [unread],
        out_specs=(vmem, vmem),
        scratch_shapes=[pltpu.VMEM((GROUP, HD, span), f32)],
        compiler_params=params,
    )(scalars, start, all_stats, *qd, kv, dv_part)

    dv = lax.all_to_all(
        dv_part.reshape(groups, rows, HD), ("y", "zh"), split_axis=0, concat_axis=0, tiled=True
    )
    value_copies = pl.pallas_call(
        sum_kernel,
        out_shape=jax.ShapeDtypeStruct((nx, rows, HD), bf16),
        in_specs=[vmem, vmem],
        out_specs=vmem,
        compiler_params=params,
    )(dv, done)
    value_x = lax.all_to_all(value_copies, "x", split_axis=0, concat_axis=0, tiled=True)
    part = wide // (tps * ny)
    term = pl.pallas_call(
        lambda *refs: weight_kernel(nx, *refs),
        out_shape=jax.ShapeDtypeStruct((ny, tps, part, HD), bf16),
        in_specs=[smem] + [vmem] * (nx + 1),
        out_specs=vmem,
        compiler_params=params,
    )(scalars, value_x, *from_x)
    pieces = lax.all_to_all(term, "y", split_axis=0, concat_axis=0, tiled=True)
    summed = jnp.sum(pieces.astype(f32), axis=0).astype(bf16)
    turned = lax.all_to_all(
        jnp.broadcast_to(summed[None], (nzh,) + summed.shape).reshape(nzh * tps, part, HD),
        ("zh",) + TP, split_axis=0, concat_axis=0, tiled=True,
    ).reshape(nzh, tps, part, HD)
    own_rows = jnp.sum(turned.astype(f32), axis=0) * (1.0 / math.sqrt(tokens))
    own_rows = own_rows.astype(bf16).transpose(1, 0, 2).reshape(part, tps * HD)
    weight_grad = spread(own_rows, ("x", "y"), nx * ny)
    dq = dq_parts[0].astype(f32)
    for d in range(1, nx):
        dq = dq + shift(dq_parts[d], "x", -d).astype(f32)
    query_grads = dq.astype(bf16)
    return (query_grads, weight_grad.reshape(wide // tps * nx, tps * HD).astype(f32))


def solution(mesh):
    fine = Mesh(mesh.devices.reshape(DIMS), AXES)
    split = P(CTX, TP)
    return jax.shard_map(
        per_device,
        mesh=fine,
        in_specs=(split, split, split, split, P(CTX, None), P()),
        out_specs=(split, P(TP, None)),
        check_vma=False,
    )
```
